512 devices in a mesh: wide: 32 (over x, z_hi, y), narrow: 16 (over z_lo, core).
Axes of the slice: x: 4, y: 4, z: 16 (z_hi: 2, z_lo: 8; z = z_hi * 8 + z_lo), core: 2. Of those that a mesh axis runs over, the one named last changes fastest.
Arguments:
- query_key: bfloat16 [16384, 32, 256], P(('wide', 'narrow')), may hold values from -27 to 27
- value_heads: bfloat16 [16384, 32, 128], P(('wide', 'narrow')), may hold values from -6 to 6
- fast_inputs: bfloat16 [16384, 16, 768], P(('wide', 'narrow')), may hold values from -6 to 6
- rate_logits: bfloat16 [16384, 16, 3], P(('wide', 'narrow')), may hold values from -4 to 4
- gate_fast: float32 [16, 256, 512], P('narrow'), may hold values from -0.375 to 0.375
- up_fast: float32 [16, 256, 512], P('narrow'), may hold values from -0.375 to 0.375
- down_fast: float32 [16, 512, 256], P('narrow'), may hold values from -0.25 to 0.25
Outputs:
- window_out: float32 [16384, 32, 128], P('wide', 'narrow')
- fast_out: float32 [16384, 16, 256], P('wide', 'narrow')
The draws below stay inside these ranges and needn't reach their ends.
All inputs are finite; a program needn't handle non-finite values.
Results may differ from the reference program's by a relative error of at most 0.009.
Values may be sent and summed in bfloat16 or wider, within the bound.
No kernel may reach another device: no remote copies, remote signals or barrier semaphores. Data moves between devices by JAX's collectives and lax.ppermute only.
A program may use at most 192 MiB of HBM per device.

```python
import math
import jax
import jax.numpy as jnp
from jax import lax

AH = 32
HD = 128
FH = 16
FD = 256
FHID = 512
WINDOW = 512
NS_STEPS = 5
TOKENS = 16384


def draw_query_key(key, part):
    key = jax.random.fold_in(key, 7)
    first = jax.random.fold_in(key, 0)
    drawn = jnp.clip(jax.random.normal(first, (TOKENS, AH, 2 * HD), jnp.float32), -6.0, 6.0)
    return drawn.astype(jnp.bfloat16)


def block_levels(stream_key, extent, shards, low, high):
    def one(position, parts):
        draws = jax.random.uniform(jax.random.fold_in(jax.random.fold_in(stream_key, 6), position), (parts,), jnp.float32, low / len(shards), high / len(shards))
        return jnp.repeat(jnp.exp(draws), extent[position] // parts).reshape((-1,) + (1,) * (len(extent) - position - 1))

    level = one(*shards[0])
    for cut in shards[1:]:
        level = level * one(*cut)
    return level


def noise(key, extent, width, most, cuts=(), held_as=jnp.bfloat16):
    drawn = width * jax.random.normal(key, extent, jnp.float32)
    if cuts:
        drawn = drawn * block_levels(key, extent, cuts, -0.22, 0.18)
    return jnp.clip(drawn, -most, most).astype(held_as)


def setup_inputs(seed: int = 0) -> dict:
    seeds = jax.random.split(jax.random.key(seed), 8)
    return {
        "query_key": draw_query_key(jax.random.fold_in(seeds[7], 71), 0),
        "value_heads": noise(seeds[1], (TOKENS, AH, HD), 1.0, 6.0, ((0, 512),)),
        "fast_inputs": noise(seeds[2], (TOKENS, FH, 3 * FD), 1.0, 6.0, ((0, 512),)),
        "rate_logits": noise(seeds[3], (TOKENS, FH, 3), 1.0, 4.0, ((0, 512),)),
        "gate_fast": noise(seeds[4], (FH, FD, FHID), FD ** -0.5, 0.375, ((0, 16),), jnp.float32),
        "up_fast": noise(seeds[5], (FH, FD, FHID), FD ** -0.5, 0.375, ((0, 16),), jnp.float32),
        "down_fast": noise(seeds[6], (FH, FHID, FD), FHID ** -0.5, 0.25, ((0, 16),), jnp.float32),
    }


coef_a = 3.4445
coef_b = -4.775
coef_c = 2.0315

def attend_block(query_rows, key_all, value_all, offset, block_index, span):
    first_row = block_index * span
    query_part = lax.dynamic_slice_in_dim(query_rows, first_row, span, 0).astype(jnp.float32)
    key_part = lax.dynamic_slice_in_dim(key_all, first_row, 2 * span, 0).astype(jnp.float32)
    value_part = lax.dynamic_slice_in_dim(value_all, first_row, 2 * span, 0).astype(jnp.float32)
    scale = 1.0 / math.sqrt(query_rows.shape[-1])
    scores = jnp.einsum('qhe,khe->hqk', query_part, key_part) * scale
    query_pos = offset + first_row + jnp.arange(span, dtype=jnp.int32)[:, None]
    key_pos = offset + first_row - span + jnp.arange(2 * span, dtype=jnp.int32)[None, :]
    distance = query_pos - key_pos
    valid_mask = (distance >= 0) & (distance < span) & (key_pos >= 0)
    scores = jnp.where(valid_mask[None], scores, -1e+30)
    row_max = lax.optimization_barrier(jnp.max(scores, axis=-1, keepdims=True))
    exp_terms = jnp.exp(scores - row_max)
    probs = (exp_terms / lax.optimization_barrier(jnp.sum(exp_terms, axis=-1, keepdims=True))).astype(jnp.bfloat16)
    return jnp.einsum('hqk,khe->qhe', probs.astype(jnp.float32), value_part).astype(jnp.float32)

def head_gradient(key_part, value_part, rates, gate_w, up_w, down_w):
    gate_bf = gate_w.astype(jnp.bfloat16)
    up_bf = up_w.astype(jnp.bfloat16)
    down_bf = down_w.astype(jnp.bfloat16)
    gate_pre = jnp.dot(key_part, gate_bf, preferred_element_type=jnp.float32)
    up_pre = jnp.dot(key_part, up_bf, preferred_element_type=jnp.float32)
    sigmoid_gate = jax.nn.sigmoid(gate_pre)
    activated = gate_pre * sigmoid_gate
    hidden = (activated * up_pre).astype(jnp.bfloat16)
    scaled_v = (rates[:, 1:2] * value_part.astype(jnp.float32)).astype(jnp.bfloat16)
    back = jnp.dot(value_part, down_bf.T, preferred_element_type=jnp.float32)
    grad_gate = (rates[:, 0:1] * back * up_pre * sigmoid_gate * (1.0 + gate_pre * (1.0 - sigmoid_gate))).astype(jnp.bfloat16)
    grad_up = (rates[:, 2:3] * back * activated).astype(jnp.bfloat16)
    delta_gate = jnp.dot(key_part.T, grad_gate, preferred_element_type=jnp.float32)
    delta_up = jnp.dot(key_part.T, grad_up, preferred_element_type=jnp.float32)
    delta_down = jnp.dot(scaled_v.T, hidden, preferred_element_type=jnp.float32)
    return jnp.stack([delta_gate, delta_up, delta_down])

def newton(ortho):
    best = lax.Precision.HIGHEST
    for _ in range(NS_STEPS):
        gram = jnp.einsum('bij,bkj->bik', ortho, ortho, precision=best)
        poly = coef_b * gram + coef_c * jnp.einsum('bij,bjk->bik', gram, gram, precision=best)
        ortho = coef_a * ortho + jnp.einsum('bij,bjk->bik', poly, ortho, precision=best)
    return ortho

def head_apply(query_part, gate_w, up_w, down_w, ortho):
    new_gate = (gate_w + ortho[0]).astype(jnp.bfloat16)
    new_up = (up_w + ortho[1]).astype(jnp.bfloat16)
    new_down = (down_w + ortho[2].T).astype(jnp.bfloat16)
    gate_pre = jnp.dot(query_part, new_gate, preferred_element_type=jnp.float32)
    up_pre = jnp.dot(query_part, new_up, preferred_element_type=jnp.float32)
    hidden = (jax.nn.silu(gate_pre) * up_pre).astype(jnp.bfloat16)
    return jnp.dot(hidden, new_down, preferred_element_type=jnp.float32)

def reference(query_key, value_heads, fast_inputs, rate_logits, gate_fast, up_fast, down_fast):
    query_rows = query_key[..., :HD]
    key_rows = query_key[..., HD:]
    padding = jnp.zeros((WINDOW, AH, HD), jnp.bfloat16)
    key_all = jnp.concatenate([padding, key_rows], axis=0)
    value_all = jnp.concatenate([padding, value_heads], axis=0)
    count = TOKENS // WINDOW

    def one_block(block_index):
        return attend_block(query_rows, key_all, value_all, 0, block_index, WINDOW)
    window_out = lax.map(one_block, jnp.arange(count, dtype=jnp.int32)).reshape(TOKENS, AH, HD)
    fast_query = jnp.moveaxis(fast_inputs[..., :FD], 1, 0)
    fast_key = jnp.moveaxis(fast_inputs[..., FD:2 * FD], 1, 0)
    fast_value = jnp.moveaxis(fast_inputs[..., 2 * FD:], 1, 0)
    rates = jnp.moveaxis(jax.nn.softplus(rate_logits.astype(jnp.float32)), 1, 0)

    def one_head(packed):
        query_part, key_part, value_part, rate_part, gate_w, up_w, down_w = packed
        summed = head_gradient(key_part, value_part, rate_part, gate_w, up_w, down_w)
        squares = lax.optimization_barrier(jnp.sum(summed * summed, axis=(1, 2), keepdims=True))
        normed = summed / jnp.sqrt(squares + 1e-06)
        ortho = newton(normed)
        return head_apply(query_part, gate_w, up_w, down_w, ortho)
    fast_heads = lax.map(one_head, (fast_query, fast_key, fast_value, rates, gate_fast, up_fast, down_fast))
    fast_out = jnp.moveaxis(fast_heads, 0, 1)
    return (window_out, fast_out)
```

```python
import math

import jax
import jax.numpy as jnp
from jax import lax
from jax.sharding import PartitionSpec as P

FD = 256
FHID = 512
WINDOW = 512
NS_STEPS = 5
LANES = 128

coef_a = 3.4445
coef_b = -4.775
coef_c = 2.0315

XS, HALVES, YS = 4, 2, 4
PLANE = XS * YS


def wide_index(x, half, y):
    return (x * HALVES + half) * YS + y


PLANES = [[wide_index(x, half, y) for x in range(XS) for y in range(YS)] for half in range(HALVES)]
SWAP = [
    (wide_index(x, half, y), wide_index(x, 1 - half, y))
    for x in range(XS)
    for half in range(HALVES)
    for y in range(YS)
]


def attend(query, key_all, value_all, offset):
    scale = 1.0 / math.sqrt(query.shape[-1])
    span = query.shape[1]
    scores = jnp.einsum("hqe,hke->hqk", query, key_all, preferred_element_type=jnp.float32) * scale
    query_pos = offset + jnp.arange(span, dtype=jnp.int32)[:, None]
    key_pos = offset - span + jnp.arange(2 * span, dtype=jnp.int32)[None, :]
    distance = query_pos - key_pos
    valid_mask = (distance >= 0) & (distance < span) & (key_pos >= 0)
    scores = jnp.where(valid_mask[None], scores, -1e30)
    row_max = jnp.max(scores, axis=-1, keepdims=True)
    exp_terms = jnp.exp(scores - row_max)
    probs = (exp_terms / jnp.sum(exp_terms, axis=-1, keepdims=True)).astype(jnp.bfloat16)
    return jnp.einsum("hqk,hke->qhe", probs, value_all, preferred_element_type=jnp.float32)


def head_gradient(key_part, value_part, rates, gate_w, up_w, down_w):
    gate_bf = gate_w.astype(jnp.bfloat16)
    up_bf = up_w.astype(jnp.bfloat16)
    down_bf = down_w.astype(jnp.bfloat16)
    gate_pre = jnp.dot(key_part, gate_bf, preferred_element_type=jnp.float32)
    up_pre = jnp.dot(key_part, up_bf, preferred_element_type=jnp.float32)
    sigmoid_gate = jax.nn.sigmoid(gate_pre)
    activated = gate_pre * sigmoid_gate
    hidden = (activated * up_pre).astype(jnp.bfloat16)
    scaled_v = (rates[:, 1:2] * value_part.astype(jnp.float32)).astype(jnp.bfloat16)
    back = jnp.dot(value_part, down_bf.T, preferred_element_type=jnp.float32)
    grad_gate = (
        rates[:, 0:1] * back * up_pre * sigmoid_gate * (1.0 + gate_pre * (1.0 - sigmoid_gate))
    ).astype(jnp.bfloat16)
    grad_up = (rates[:, 2:3] * back * activated).astype(jnp.bfloat16)
    delta_gate = jnp.dot(key_part.T, grad_gate, preferred_element_type=jnp.float32)
    delta_up = jnp.dot(key_part.T, grad_up, preferred_element_type=jnp.float32)
    delta_down = jnp.dot(scaled_v.T, hidden, preferred_element_type=jnp.float32)
    return jnp.stack([delta_gate, delta_up, delta_down])


def block_sum(grads):
    rows = FD // PLANE
    most = jnp.max(jnp.abs(grads), axis=(1, 2))
    power = jnp.floor(jnp.log2(jnp.maximum(most, 1e-30)))
    scaled = (grads * jnp.exp2(13.0 - power)[:, None, None]).astype(jnp.float16)
    pieces = scaled.reshape(3, PLANE, rows, FHID // LANES, LANES).transpose(1, 0, 3, 2, 4)
    pieces = pieces.reshape(PLANE, 3 * FHID // LANES * rows, LANES)
    count = pieces.shape[1]
    tag = jnp.zeros((16, LANES), jnp.float16).at[:3, :].set(
        jnp.broadcast_to(power.astype(jnp.float16)[:, None], (3, LANES))
    )
    sent = jnp.concatenate([pieces, jnp.broadcast_to(tag, (PLANE, 16, LANES))], axis=1)
    got = lax.all_to_all(sent, "wide", 0, 0, tiled=True, axis_index_groups=PLANES)
    powers = got[:, count : count + 3, 0].astype(jnp.float32)
    top = jnp.max(powers, axis=0)
    parts = got[:, :count].astype(jnp.float32).reshape(PLANE, 3, -1, LANES)
    half = jnp.sum(parts * (jnp.exp2(powers - top) * 0.0625)[:, :, None, None], axis=0)
    tag = jnp.zeros((16, LANES), jnp.float16).at[:3, :].set(
        jnp.broadcast_to(top.astype(jnp.float16)[:, None], (3, LANES))
    )
    sent = jnp.concatenate([half.astype(jnp.float16).reshape(count, LANES), tag], axis=0)
    other = lax.ppermute(sent, "wide", SWAP)
    other_top = other[count : count + 3, 0].astype(jnp.float32)
    both = jnp.maximum(top, other_top)
    whole = half * (jnp.exp2(top - both) * 0.5)[:, None, None]
    whole = whole + other[:count].astype(jnp.float32).reshape(3, -1, LANES) * (
        jnp.exp2(other_top - both) * 0.5
    )[:, None, None]
    every = lax.all_gather(
        whole.astype(jnp.float16).reshape(count, LANES), "wide", axis_index_groups=PLANES
    )
    every = every.reshape(PLANE, 3, FHID // LANES, rows, LANES).transpose(1, 0, 3, 2, 4)
    return every.reshape(3, FD, FHID).astype(jnp.float32) * jnp.exp2(both - 8.0)[:, None, None]


def newton(ortho):
    best = lax.Precision.HIGH
    for _ in range(NS_STEPS):
        gram = jnp.einsum("bij,bkj->bik", ortho, ortho, precision=best)
        poly = coef_b * gram + coef_c * jnp.einsum("bij,bjk->bik", gram, gram, precision=best)
        ortho = coef_a * ortho + jnp.einsum("bij,bjk->bik", poly, ortho, precision=best)
    return ortho


def head_apply(query_part, gate_w, up_w, down_w, ortho):
    new_gate = (gate_w + ortho[0]).astype(jnp.bfloat16)
    new_up = (up_w + ortho[1]).astype(jnp.bfloat16)
    new_down = (down_w + ortho[2].T).astype(jnp.bfloat16)
    gate_pre = jnp.dot(query_part, new_gate, preferred_element_type=jnp.float32)
    up_pre = jnp.dot(query_part, new_up, preferred_element_type=jnp.float32)
    hidden = (jax.nn.silu(gate_pre) * up_pre).astype(jnp.bfloat16)
    return jnp.dot(hidden, new_down, preferred_element_type=jnp.float32)


def per_device(query_key, value_heads, fast_inputs, rate_logits, gate_fast, up_fast, down_fast):
    group = lax.axis_size("narrow")
    rows = query_key.shape[0]
    own = query_key.shape[1] // group
    span = rows * group
    pair = query_key.reshape(rows, group, own, 2, LANES)
    query = pair[:, :, :, 0].transpose(1, 2, 0, 3)
    key = pair[:, :, :, 1].transpose(1, 2, 0, 3)
    value = value_heads.reshape(rows, group, own, LANES).transpose(1, 2, 0, 3)
    fast = fast_inputs.reshape(rows, group, 6, LANES).transpose(1, 2, 0, 3)
    logits = jnp.pad(rate_logits.transpose(1, 2, 0), ((0, 0), (0, 13), (0, LANES - rows)))
    first = jnp.concatenate([key, value, fast[:, 2:]], axis=1)
    blocks = first.shape[1]
    first = jnp.concatenate([first.reshape(group, blocks * rows, LANES), logits], axis=1)
    second = jnp.concatenate([query, fast[:, :2]], axis=1)

    first = lax.all_to_all(first, "narrow", 0, 0, tiled=True)
    second = lax.all_to_all(second, "narrow", 0, 0, tiled=True)

    parts = first[:, : blocks * rows].reshape(group, blocks, rows, LANES)
    logit_rows = first[:, blocks * rows : blocks * rows + 3, :rows]
    rates = jax.nn.softplus(logit_rows.transpose(0, 2, 1).reshape(span, 3).astype(jnp.float32))
    fast_key = parts[:, 4:6].transpose(0, 2, 1, 3).reshape(span, FD)
    fast_value = parts[:, 6:8].transpose(0, 2, 1, 3).reshape(span, FD)
    grads = head_gradient(fast_key, fast_value, rates, gate_fast[0], up_fast[0], down_fast[0])

    tail = parts[:, :4]
    devices = lax.axis_size("wide")
    earlier = lax.ppermute(tail, "wide", [(i, i + 1) for i in range(devices - 1)])
    near = tail.transpose(1, 0, 2, 3).reshape(4, span, LANES)
    far = earlier.transpose(1, 0, 2, 3).reshape(4, span, LANES)
    both = jnp.concatenate([far, near], axis=1)

    summed = block_sum(grads)
    squares = jnp.sum(summed * summed, axis=(1, 2), keepdims=True)
    ortho = newton(summed / jnp.sqrt(squares + 1e-06))

    chunks = second.transpose(1, 0, 2, 3).reshape(4, span, LANES)
    offset = lax.axis_index("wide") * span
    window_out = attend(chunks[:2], both[:2], both[2:], offset)
    fast_query = second[:, 2:].transpose(0, 2, 1, 3).reshape(span, FD)
    fast_out = head_apply(fast_query, gate_fast[0], up_fast[0], down_fast[0], ortho)
    return (window_out, fast_out[:, None, :])


def solution(mesh):
    return jax.shard_map(
        per_device,
        mesh=mesh,
        in_specs=(
            P(("wide", "narrow"), None, None),
            P(("wide", "narrow"), None, None),
            P(("wide", "narrow"), None, None),
            P(("wide", "narrow"), None, None),
            P("narrow", None, None),
            P("narrow", None, None),
            P("narrow", None, None),
        ),
        out_specs=(P("wide", "narrow", None), P("wide", "narrow", None)),
        check_vma=False,
    )
```

```python
import math

import jax
import jax.numpy as jnp
from jax import lax
from jax.experimental import pallas as pl
from jax.experimental.pallas import tpu as pltpu
from jax.sharding import PartitionSpec as P

FD = 256
FHID = 512
WINDOW = 512
NS_STEPS = 5
LANES = 128
TOK = 32

coef_a = 3.4445
coef_b = -4.775
coef_c = 2.0315

XS, HALVES, YS = 4, 2, 4
PLANE = XS * YS
VMEM_LIMIT = 48 * 1024 * 1024


def dot(a, b, dims=((1,), (0,))):
    return lax.dot_general(a, b, (dims, ((), ())), preferred_element_type=jnp.float32)


def block_rows(ref, index, count):
    group = ref.shape[0]
    parts = [
        ref[:, (index + i) * TOK : (index + i + 1) * TOK, :].reshape(group * TOK, LANES)
        for i in range(count)
    ]
    return parts[0] if count == 1 else jnp.concatenate(parts, axis=1)


def gradient_kernel(first, gate, up, down, out):
    group = first.shape[0]
    span = group * TOK
    logits = first[:, 8 * TOK : 8 * TOK + 16, :].astype(jnp.float32)
    rate_blocks = []
    for source in range(group):
        turned = logits[source].T[:TOK]
        rate_blocks.append(jnp.maximum(turned, 0.0) + jnp.log1p(jnp.exp(-jnp.abs(turned))))
    rates = jnp.concatenate(rate_blocks, axis=0)
    key = block_rows(first, 4, 2)
    value = block_rows(first, 6, 2)
    gate_bf = gate[...].astype(jnp.bfloat16)
    up_bf = up[...].astype(jnp.bfloat16)
    down_bf = down[...].astype(jnp.bfloat16)
    totals = [None, None, None]
    half = span // 2
    for part in range(2):
        rows = slice(part * half, (part + 1) * half)
        key_part, value_part, rate = key[rows], value[rows], rates[rows]
        gate_pre = dot(key_part, gate_bf)
        up_pre = dot(key_part, up_bf)
        back = dot(value_part, down_bf, ((1,), (1,)))
        sigmoid_gate = 1.0 / (1.0 + jnp.exp(-gate_pre))
        activated = gate_pre * sigmoid_gate
        hidden = (activated * up_pre).astype(jnp.bfloat16)
        scaled_v = (rate[:, 1:2] * value_part.astype(jnp.float32)).astype(jnp.bfloat16)
        grad_gate = (
            rate[:, 0:1] * back * up_pre * sigmoid_gate * (1.0 + gate_pre * (1.0 - sigmoid_gate))
        ).astype(jnp.bfloat16)
        grad_up = (rate[:, 2:3] * back * activated).astype(jnp.bfloat16)
        fresh = (
            dot(key_part, grad_gate, ((0,), (0,))),
            dot(key_part, grad_up, ((0,), (0,))),
            dot(scaled_v, hidden, ((0,), (0,))),
        )
        totals = [new if old is None else old + new for old, new in zip(totals, fresh)]
    rows = FD // PLANE
    row = lax.broadcasted_iota(jnp.int32, (16, LANES), 0)
    tag = jnp.zeros((16, LANES), jnp.float32)
    for matrix, total in enumerate(totals):
        most = jnp.max(jnp.max(jnp.abs(total), axis=0, keepdims=True), axis=1, keepdims=True)
        power = jnp.floor(jnp.log(jnp.maximum(most, 1e-30)) * 1.4426950408889634)
        scaled = total * jnp.exp((13.0 - power) * 0.6931471805599453)
        tag = jnp.where(row == matrix, power, tag)
        for column in range(FHID // LANES):
            start = (matrix * (FHID // LANES) + column) * rows
            out[:, start : start + rows, :] = scaled[
                :, column * LANES : (column + 1) * LANES
            ].reshape(PLANE, rows, LANES)
    out[:, 3 * FHID // LANES * rows :, :] = jnp.broadcast_to(tag[None], (PLANE, 16, LANES))


def attention_kernel(place, first, earlier, second, out):
    span = first.shape[0] * TOK
    scale = 1.0 / math.sqrt(LANES)
    tile = 128
    reach = span + tile
    row = lax.broadcasted_iota(jnp.int32, (tile, reach), 0)
    col = lax.broadcasted_iota(jnp.int32, (tile, reach), 1)
    band = (col > row) & (col - row <= span)
    begin = jnp.where(place[0] == 0, span, 0)
    heads = second.shape[1] // TOK // 2
    for head in range(heads):
        query = block_rows(second, head, 1)
        key = jnp.concatenate([block_rows(earlier, head, 1), block_rows(first, head, 1)], axis=0)
        value = jnp.concatenate(
            [block_rows(earlier, heads + head, 1), block_rows(first, heads + head, 1)], axis=0
        )
        for step in range(span // tile):
            low = step * tile
            scores = dot(query[low : low + tile], key[low : low + reach], ((1,), (1,))) * scale
            keep = band & (col + low >= begin)
            scores = jnp.where(keep, scores, -1e30)
            terms = jnp.exp(scores - jnp.max(scores, axis=1, keepdims=True))
            probs = (terms * (1.0 / jnp.sum(terms, axis=1, keepdims=True))).astype(jnp.bfloat16)
            out[pl.ds(low * heads + head, tile, stride=heads), :] = dot(
                probs, value[low : low + reach]
            )


def split(a):
    high = a.astype(jnp.bfloat16)
    return high, (a - high.astype(jnp.float32)).astype(jnp.bfloat16)


def orthogonal(ortho_all):
    for _ in range(NS_STEPS):
        grams, polys, nexts = [], [], []
        halves = [split(ortho) for ortho in ortho_all]
        for high, low in halves:
            cross = dot(high, low, ((1,), (1,)))
            grams.append(dot(high, high, ((1,), (1,))) + (cross + cross.T))
        for gram in grams:
            high, low = split(gram)
            square = dot(high, high) + (dot(high, low) + dot(low, high))
            polys.append(coef_b * gram + coef_c * square)
        for ortho, poly, (high, low) in zip(ortho_all, polys, halves):
            top, rest = split(poly)
            nexts.append(coef_a * ortho + (dot(top, high) + (dot(top, low) + dot(rest, high))))
        ortho_all = nexts
    return ortho_all


def apply_kernel(powers, every, gate, up, down, second, out):
    rows = FD // PLANE
    starts = []
    for matrix in range(3):
        columns = []
        for column in range(FHID // LANES):
            start = (matrix * (FHID // LANES) + column) * rows
            columns.append(every[:, start : start + rows, :].reshape(FD, LANES))
        total = jnp.concatenate(columns, axis=1)
        squares = jnp.sum(jnp.sum(total * total, axis=0, keepdims=True), axis=1, keepdims=True)
        factor = powers[matrix : matrix + 1, 0:1]
        starts.append(total * (factor / jnp.sqrt(squares * factor * factor + 1e-6)))
    ortho = orthogonal(starts)
    new_gate = (gate[...] + ortho[0]).astype(jnp.bfloat16)
    new_up = (up[...] + ortho[1]).astype(jnp.bfloat16)
    new_down = (down[...] + ortho[2].T).astype(jnp.bfloat16)
    query = block_rows(second, 2, 2)
    gate_pre = dot(query, new_gate)
    up_pre = dot(query, new_up)
    hidden = (gate_pre * (1.0 / (1.0 + jnp.exp(-gate_pre))) * up_pre).astype(jnp.bfloat16)
    result = dot(hidden, new_down)
    span = result.shape[0]
    for column in range(FD // LANES):
        out[pl.ds(column, span, stride=FD // LANES), :] = result[
            :, column * LANES : (column + 1) * LANES
        ]


def call(kernel, shape, operands, flops, scalars=0):
    vmem = pl.BlockSpec(memory_space=pltpu.VMEM)
    smem = pl.BlockSpec(memory_space=pltpu.SMEM)
    return pl.pallas_call(
        kernel,
        out_shape=jax.ShapeDtypeStruct(shape, jnp.float32),
        in_specs=[smem] * scalars + [vmem] * (len(operands) - scalars),
        out_specs=vmem,
        compiler_params=pltpu.CompilerParams(vmem_limit_bytes=VMEM_LIMIT),
        cost_estimate=pl.CostEstimate(flops=flops, bytes_accessed=4 << 20, transcendentals=0),
    )(*operands)


def wide_index(x, half, y):
    return (x * HALVES + half) * YS + y


PLANES = [[wide_index(x, half, y) for x in range(XS) for y in range(YS)] for half in range(HALVES)]
SWAP = [
    (wide_index(x, half, y), wide_index(x, 1 - half, y))
    for x in range(XS)
    for half in range(HALVES)
    for y in range(YS)
]


def tag_rows(power):
    wide = jnp.broadcast_to(power.astype(jnp.float16)[:, None], (3, LANES))
    return jnp.concatenate([wide, jnp.zeros((13, LANES), jnp.float16)], axis=0)


def per_device(query_key, value_heads, fast_inputs, rate_logits, gate_fast, up_fast, down_fast):
    group = lax.axis_size("narrow")
    rows = query_key.shape[0]
    own = query_key.shape[1] // group
    span = rows * group
    pair = query_key.reshape(rows, group, own, 2, LANES)
    query = pair[:, :, :, 0].transpose(1, 2, 0, 3)
    key = pair[:, :, :, 1].transpose(1, 2, 0, 3)
    value = value_heads.reshape(rows, group, own, LANES).transpose(1, 2, 0, 3)
    fast = fast_inputs.reshape(rows, group, 6, LANES).transpose(1, 2, 0, 3)
    logits = jnp.pad(rate_logits.transpose(1, 2, 0), ((0, 0), (0, 13), (0, LANES - rows)))
    first = jnp.concatenate([key, value, fast[:, 2:]], axis=1)
    blocks = first.shape[1]
    first = jnp.concatenate([first.reshape(group, blocks * rows, LANES), logits], axis=1)
    second = jnp.concatenate([query, fast[:, :2]], axis=1).reshape(group, 4 * rows, LANES)

    first = lax.all_to_all(first, "narrow", 0, 0, tiled=True)
    devices = lax.axis_size("wide")
    earlier = lax.ppermute(
        first[:, : 4 * rows], "wide", [(i, i + 1) for i in range(devices - 1)]
    )

    weights = (gate_fast[0], up_fast[0], down_fast[0])
    count = 3 * FHID // LANES * FD // PLANE
    pieces = call(gradient_kernel, (PLANE, count + 16, LANES), (first, *weights), 1 << 30)
    got = lax.all_to_all(
        pieces.astype(jnp.float16), "wide", 0, 0, tiled=True, axis_index_groups=PLANES
    )
    second, got = lax.optimization_barrier((second, got))
    second = lax.all_to_all(second, "narrow", 0, 0, tiled=True)
    powers = got[:, count : count + 3, 0].astype(jnp.float32)
    top = jnp.max(powers, axis=0)
    parts = got[:, :count].astype(jnp.float32).reshape(PLANE, 3, -1, LANES)
    half = jnp.sum(parts * (jnp.exp2(powers - top) * 0.0625)[:, :, None, None], axis=0)
    sent = jnp.concatenate([half.astype(jnp.float16).reshape(count, LANES), tag_rows(top)], axis=0)
    other = lax.ppermute(sent, "wide", SWAP)
    other_top = other[count : count + 3, 0].astype(jnp.float32)
    both = jnp.maximum(top, other_top)
    whole = half * (jnp.exp2(top - both) * 0.5)[:, None, None]
    whole = whole + other[:count].astype(jnp.float32).reshape(3, -1, LANES) * (
        jnp.exp2(other_top - both) * 0.5
    )[:, None, None]
    every = lax.all_gather(
        whole.astype(jnp.float16).reshape(count, LANES), "wide", axis_index_groups=PLANES
    )
    factors = jnp.broadcast_to(
        jnp.concatenate([jnp.exp2(both - 8.0), jnp.zeros((5,), jnp.float32)])[:, None], (8, LANES)
    )
    fast_out = call(
        apply_kernel,
        (span * FD // LANES, LANES),
        (factors, every.astype(jnp.float32), *weights, second),
        10 << 30,
    )
    earlier, fast_out = lax.optimization_barrier((earlier, fast_out))
    place = lax.axis_index("wide").reshape(1)
    window_out = call(
        attention_kernel, (span * own, LANES), (place, first, earlier, second), 1 << 30, 1
    )
    return (window_out.reshape(span, own, LANES), fast_out.reshape(span, 1, FD))


def solution(mesh):
    return jax.shard_map(
        per_device,
        mesh=mesh,
        in_specs=(
            P(("wide", "narrow"), None, None),
            P(("wide", "narrow"), None, None),
            P(("wide", "narrow"), None, None),
            P(("wide", "narrow"), None, None),
            P("narrow", None, None),
            P("narrow", None, None),
            P("narrow", None, None),
        ),
        out_specs=(P("wide", "narrow", None), P("wide", "narrow", None)),
        check_vma=False,
    )
```

```python
import math

import jax
import jax.numpy as jnp
from jax import lax
from jax.experimental import pallas as pl
from jax.experimental.pallas import tpu as pltpu
from jax.sharding import PartitionSpec as P

FD = 256
FHID = 512
WINDOW = 512
NS_STEPS = 5
LANES = 128
TOK = 32

coef_a = 3.4445
coef_b = -4.775
coef_c = 2.0315

XS, HALVES, YS = 4, 2, 4
PLANE = XS * YS
VMEM_LIMIT = 48 * 1024 * 1024


def dot(a, b, dims=((1,), (0,))):
    return lax.dot_general(a, b, (dims, ((), ())), preferred_element_type=jnp.float32)


def block_rows(ref, index, count):
    group = ref.shape[0]
    parts = [
        ref[:, (index + i) * TOK : (index + i + 1) * TOK, :].reshape(group * TOK, LANES)
        for i in range(count)
    ]
    return parts[0] if count == 1 else jnp.concatenate(parts, axis=1)


def gradient_kernel(first, gate, up, down, out):
    group = first.shape[0]
    span = group * TOK
    logits = first[:, 6 * TOK : 6 * TOK + 16, :].astype(jnp.float32)
    rate_blocks = []
    for source in range(group):
        turned = logits[source].T[:TOK]
        rate_blocks.append(jnp.maximum(turned, 0.0) + jnp.log1p(jnp.exp(-jnp.abs(turned))))
    rates = jnp.concatenate(rate_blocks, axis=0)
    key = block_rows(first, 0, 2)
    value = block_rows(first, 2, 2)
    gate_bf = gate[...].astype(jnp.bfloat16)
    up_bf = up[...].astype(jnp.bfloat16)
    down_bf = down[...].astype(jnp.bfloat16)
    totals = [None, None, None]
    half = span // 2
    for part in range(2):
        rows = slice(part * half, (part + 1) * half)
        key_part, value_part, rate = key[rows], value[rows], rates[rows]
        gate_pre = dot(key_part, gate_bf)
        up_pre = dot(key_part, up_bf)
        back = dot(value_part, down_bf, ((1,), (1,)))
        sigmoid_gate = 1.0 / (1.0 + jnp.exp(-gate_pre))
        activated = gate_pre * sigmoid_gate
        hidden = (activated * up_pre).astype(jnp.bfloat16)
        scaled_v = (rate[:, 1:2] * value_part.astype(jnp.float32)).astype(jnp.bfloat16)
        grad_gate = (
            rate[:, 0:1] * back * up_pre * sigmoid_gate * (1.0 + gate_pre * (1.0 - sigmoid_gate))
        ).astype(jnp.bfloat16)
        grad_up = (rate[:, 2:3] * back * activated).astype(jnp.bfloat16)
        fresh = (
            dot(key_part, grad_gate, ((0,), (0,))),
            dot(key_part, grad_up, ((0,), (0,))),
            dot(scaled_v, hidden, ((0,), (0,))),
        )
        totals = [new if old is None else old + new for old, new in zip(totals, fresh)]
    rows = FD // PLANE
    row = lax.broadcasted_iota(jnp.int32, (16, LANES), 0)
    tag = jnp.zeros((16, LANES), jnp.float32)
    for matrix, total in enumerate(totals):
        most = jnp.max(jnp.max(jnp.abs(total), axis=0, keepdims=True), axis=1, keepdims=True)
        power = jnp.floor(jnp.log(jnp.maximum(most, 1e-30)) * 1.4426950408889634)
        scaled = total * jnp.exp((13.0 - power) * 0.6931471805599453)
        tag = jnp.where(row == matrix, power, tag)
        for column in range(FHID // LANES):
            start = (matrix * (FHID // LANES) + column) * rows
            out[:, start : start + rows, :] = scaled[
                :, column * LANES : (column + 1) * LANES
            ].reshape(PLANE, rows, LANES)
    out[:, 3 * FHID // LANES * rows :, :] = jnp.broadcast_to(tag[None], (PLANE, 16, LANES))


def attention_kernel(
    place, first, second, earlier_key, earlier_value, earlier_second, third, out
):
    span = first.shape[0] * TOK
    scale = 1.0 / math.sqrt(LANES)
    tile = 128
    reach = span + tile
    row = lax.broadcasted_iota(jnp.int32, (tile, reach), 0)
    col = lax.broadcasted_iota(jnp.int32, (tile, reach), 1)
    band = (col > row) & (col - row <= span)
    begin = jnp.where(place[0] == 0, span, 0)
    heads = 2
    sources = (
        (earlier_key, 0, earlier_value, 0, first, 4),
        (earlier_second, 0, earlier_second, 1, second, 0),
    )
    for head, (far_key, far, far_value, other, near, at) in enumerate(sources):
        query = block_rows(third, head, 1)
        key = jnp.concatenate([block_rows(far_key, far, 1), block_rows(near, at, 1)], axis=0)
        value = jnp.concatenate(
            [block_rows(far_value, other, 1), block_rows(near, at + 1, 1)], axis=0
        )
        for step in range(span // tile):
            low = step * tile
            scores = dot(query[low : low + tile], key[low : low + reach], ((1,), (1,))) * scale
            keep = band & (col + low >= begin)
            scores = jnp.where(keep, scores, -1e30)
            terms = jnp.exp(scores - jnp.max(scores, axis=1, keepdims=True))
            probs = (terms * (1.0 / jnp.sum(terms, axis=1, keepdims=True))).astype(jnp.bfloat16)
            out[pl.ds(low * heads + head, tile, stride=heads), :] = dot(
                probs, value[low : low + reach]
            )


def split(a):
    high = a.astype(jnp.bfloat16)
    return high, (a - high.astype(jnp.float32)).astype(jnp.bfloat16)


def orthogonal(ortho_all):
    for _ in range(NS_STEPS):
        grams, polys, nexts = [], [], []
        halves = [split(ortho) for ortho in ortho_all]
        for high, low in halves:
            cross = dot(high, low, ((1,), (1,)))
            grams.append(dot(high, high, ((1,), (1,))) + (cross + cross.T))
        for gram in grams:
            high, low = split(gram)
            square = dot(high, high) + (dot(high, low) + dot(low, high))
            polys.append(coef_b * gram + coef_c * square)
        for ortho, poly, (high, low) in zip(ortho_all, polys, halves):
            top, rest = split(poly)
            nexts.append(coef_a * ortho + (dot(top, high) + (dot(top, low) + dot(rest, high))))
        ortho_all = nexts
    return ortho_all


def update_kernel(powers, every, gate, up, down, new_gate, new_up, new_down):
    rows = FD // PLANE
    starts = []
    for matrix in range(3):
        columns = []
        for column in range(FHID // LANES):
            start = (matrix * (FHID // LANES) + column) * rows
            columns.append(every[:, start : start + rows, :].reshape(FD, LANES))
        total = jnp.concatenate(columns, axis=1)
        squares = jnp.sum(jnp.sum(total * total, axis=0, keepdims=True), axis=1, keepdims=True)
        factor = powers[matrix : matrix + 1, 0:1]
        starts.append(total * (factor / jnp.sqrt(squares * factor * factor + 1e-6)))
    ortho = orthogonal(starts)
    new_gate[...] = (gate[...] + ortho[0]).astype(jnp.bfloat16)
    new_up[...] = (up[...] + ortho[1]).astype(jnp.bfloat16)
    new_down[...] = (down[...] + ortho[2].T).astype(jnp.bfloat16)


def apply_kernel(third, new_gate, new_up, new_down, out):
    query = block_rows(third, 2, 2)
    gate_pre = dot(query, new_gate[...])
    up_pre = dot(query, new_up[...])
    hidden = (gate_pre * (1.0 / (1.0 + jnp.exp(-gate_pre))) * up_pre).astype(jnp.bfloat16)
    result = dot(hidden, new_down[...])
    span = result.shape[0]
    for column in range(FD // LANES):
        out[pl.ds(column, span, stride=FD // LANES), :] = result[
            :, column * LANES : (column + 1) * LANES
        ]


def call(kernel, shapes, operands, flops, scalars=0):
    vmem = pl.BlockSpec(memory_space=pltpu.VMEM)
    smem = pl.BlockSpec(memory_space=pltpu.SMEM)
    return pl.pallas_call(
        kernel,
        out_shape=[jax.ShapeDtypeStruct(shape, dtype) for shape, dtype in shapes],
        in_specs=[smem] * scalars + [vmem] * (len(operands) - scalars),
        out_specs=[vmem] * len(shapes),
        compiler_params=pltpu.CompilerParams(vmem_limit_bytes=VMEM_LIMIT),
        cost_estimate=pl.CostEstimate(flops=flops, bytes_accessed=1 << 20, transcendentals=0),
    )(*operands)


def wide_index(x, half, y):
    return (x * HALVES + half) * YS + y


PLANES = [[wide_index(x, half, y) for x in range(XS) for y in range(YS)] for half in range(HALVES)]
SWAP = [
    (wide_index(x, half, y), wide_index(x, 1 - half, y))
    for x in range(XS)
    for half in range(HALVES)
    for y in range(YS)
]


FLOPS = 1 << 20


def tag_rows(power):
    wide = jnp.broadcast_to(power.astype(jnp.float16)[:, None], (3, LANES))
    return jnp.concatenate([wide, jnp.zeros((13, LANES), jnp.float16)], axis=0)


def per_device(query_key, value_heads, fast_inputs, rate_logits, gate_fast, up_fast, down_fast):
    group = lax.axis_size("narrow")
    rows = query_key.shape[0]
    own = query_key.shape[1] // group
    span = rows * group
    pair = query_key.reshape(rows, group, own, 2, LANES)
    query = pair[:, :, :, 0].transpose(1, 2, 0, 3)
    key = pair[:, :, :, 1].transpose(1, 2, 0, 3)
    value = value_heads.reshape(rows, group, own, LANES).transpose(1, 2, 0, 3)
    fast = fast_inputs.reshape(rows, group, 6, LANES).transpose(1, 2, 0, 3)
    logits = jnp.pad(rate_logits.transpose(1, 2, 0), ((0, 0), (0, 13), (0, LANES - rows)))
    pairs = jnp.stack([key, value], axis=2)
    first = jnp.concatenate([fast[:, 2:], pairs[:, 0]], axis=1).reshape(group, 6 * rows, LANES)
    first = jnp.concatenate([first, logits], axis=1)
    second = pairs[:, 1].reshape(group, 2 * rows, LANES)
    third = jnp.concatenate([query, fast[:, :2]], axis=1).reshape(group, 4 * rows, LANES)
    float32, bfloat16 = jnp.float32, jnp.bfloat16
    devices = lax.axis_size("wide")
    later = [(i, i + 1) for i in range(devices - 1)]

    first = lax.all_to_all(first, "narrow", 0, 0, tiled=True)
    earlier_key = lax.ppermute(first[:, 4 * rows : 5 * rows], "wide", later)
    earlier_value = lax.ppermute(first[:, 5 * rows : 6 * rows], "wide", later)

    weights = (gate_fast[0], up_fast[0], down_fast[0])
    count = 3 * FHID // LANES * FD // PLANE
    (pieces,) = call(
        gradient_kernel, [((PLANE, count + 16, LANES), float32)], (first, *weights), FLOPS
    )
    got = lax.all_to_all(
        pieces.astype(jnp.float16), "wide", 0, 0, tiled=True, axis_index_groups=PLANES
    )
    second, got, earlier_key = lax.optimization_barrier((second, got, earlier_key))
    second = lax.all_to_all(second, "narrow", 0, 0, tiled=True)
    powers = got[:, count : count + 3, 0].astype(float32)
    top = jnp.max(powers, axis=0)
    parts = got[:, :count].astype(float32).reshape(PLANE, 3, -1, LANES)
    half = jnp.sum(parts * (jnp.exp2(powers - top) * 0.0625)[:, :, None, None], axis=0)
    sent = jnp.concatenate([half.astype(jnp.float16).reshape(count, LANES), tag_rows(top)], axis=0)
    other = lax.ppermute(sent, "wide", SWAP)
    third, second, other, earlier_value = lax.optimization_barrier(
        (third, second, other, earlier_value)
    )
    third = lax.all_to_all(third, "narrow", 0, 0, tiled=True)
    earlier_second = lax.ppermute(second, "wide", later)
    other_top = other[count : count + 3, 0].astype(float32)
    both = jnp.maximum(top, other_top)
    whole = half * (jnp.exp2(top - both) * 0.5)[:, None, None]
    whole = whole + other[:count].astype(float32).reshape(3, -1, LANES) * (
        jnp.exp2(other_top - both) * 0.5
    )[:, None, None]
    whole = whole.astype(jnp.float16).reshape(count, LANES)
    every = lax.all_gather(whole, "wide", axis_index_groups=PLANES)
    factors = jnp.broadcast_to(
        jnp.concatenate([jnp.exp2(both - 8.0), jnp.zeros((5,), float32)])[:, None], (8, LANES)
    )
    fresh = call(
        update_kernel,
        [((FD, FHID), bfloat16), ((FD, FHID), bfloat16), ((FHID, FD), bfloat16)],
        (factors, every.astype(float32), *weights),
        FLOPS,
    )
    (fast_out,) = call(
        apply_kernel, [((span * FD // LANES, LANES), float32)], (third, *fresh), FLOPS
    )
    place = lax.axis_index("wide").reshape(1)
    earlier_second, fast_out = lax.optimization_barrier((earlier_second, fast_out))
    (window_out,) = call(
        attention_kernel,
        [((span * own, LANES), float32)],
        (place, first, second, earlier_key, earlier_value, earlier_second, third),
        FLOPS,
        1,
    )
    return (window_out.reshape(span, own, LANES), fast_out.reshape(span, 1, FD))


def solution(mesh):
    return jax.shard_map(
        per_device,
        mesh=mesh,
        in_specs=(
            P(("wide", "narrow"), None, None),
            P(("wide", "narrow"), None, None),
            P(("wide", "narrow"), None, None),
            P(("wide", "narrow"), None, None),
            P("narrow", None, None),
            P("narrow", None, None),
            P("narrow", None, None),
        ),
        out_specs=(P("wide", "narrow", None), P("wide", "narrow", None)),
        check_vma=False,
    )
```

```python
import math

import jax
import jax.numpy as jnp
from jax import lax
from jax.experimental import pallas as pl
from jax.experimental.pallas import tpu as pltpu
from jax.sharding import PartitionSpec as P

FD = 256
FHID = 512
WINDOW = 512
NS_STEPS = 5
LANES = 128
TOK = 32

coef_a = 3.4445
coef_b = -4.775
coef_c = 2.0315

XS, HALVES, YS = 4, 2, 4
PLANE = XS * YS
VMEM_LIMIT = 48 * 1024 * 1024


def dot(a, b, dims=((1,), (0,))):
    return lax.dot_general(a, b, (dims, ((), ())), preferred_element_type=jnp.float32)


def block_rows(ref, index, count):
    group = ref.shape[0]
    parts = [
        ref[:, (index + i) * TOK : (index + i + 1) * TOK, :].reshape(group * TOK, LANES)
        for i in range(count)
    ]
    return parts[0] if count == 1 else jnp.concatenate(parts, axis=1)


def gradient_kernel(first, gate, up, down, out):
    group = first.shape[0]
    span = group * TOK
    logits = first[:, 12 * TOK : 12 * TOK + 16, :].astype(jnp.float32)
    rate_blocks = []
    for source in range(group):
        turned = logits[source].T[:TOK]
        rate_blocks.append(jnp.maximum(turned, 0.0) + jnp.log1p(jnp.exp(-jnp.abs(turned))))
    rates = jnp.concatenate(rate_blocks, axis=0)
    key = block_rows(first, 4, 2)
    value = block_rows(first, 6, 2)
    gate_bf = gate[...].astype(jnp.bfloat16)
    up_bf = up[...].astype(jnp.bfloat16)
    down_bf = down[...].astype(jnp.bfloat16)
    totals = [None, None, None]
    half = span // 2
    for part in range(2):
        rows = slice(part * half, (part + 1) * half)
        key_part, value_part, rate = key[rows], value[rows], rates[rows]
        gate_pre = dot(key_part, gate_bf)
        up_pre = dot(key_part, up_bf)
        back = dot(value_part, down_bf, ((1,), (1,)))
        sigmoid_gate = 1.0 / (1.0 + jnp.exp(-gate_pre))
        activated = gate_pre * sigmoid_gate
        hidden = (activated * up_pre).astype(jnp.bfloat16)
        scaled_v = (rate[:, 1:2] * value_part.astype(jnp.float32)).astype(jnp.bfloat16)
        grad_gate = (
            rate[:, 0:1] * back * up_pre * sigmoid_gate * (1.0 + gate_pre * (1.0 - sigmoid_gate))
        ).astype(jnp.bfloat16)
        grad_up = (rate[:, 2:3] * back * activated).astype(jnp.bfloat16)
        fresh = (
            dot(key_part, grad_gate, ((0,), (0,))),
            dot(key_part, grad_up, ((0,), (0,))),
            dot(scaled_v, hidden, ((0,), (0,))),
        )
        totals = [new if old is None else old + new for old, new in zip(totals, fresh)]
    rows = FD // PLANE
    row = lax.broadcasted_iota(jnp.int32, (16, LANES), 0)
    tag = jnp.zeros((16, LANES), jnp.float32)
    for matrix, total in enumerate(totals):
        most = jnp.max(jnp.max(jnp.abs(total), axis=0, keepdims=True), axis=1, keepdims=True)
        power = jnp.floor(jnp.log(jnp.maximum(most, 1e-30)) * 1.4426950408889634)
        scaled = total * jnp.exp((13.0 - power) * 0.6931471805599453)
        tag = jnp.where(row == matrix, power, tag)
        for column in range(FHID // LANES):
            start = (matrix * (FHID // LANES) + column) * rows
            out[:, start : start + rows, :] = scaled[
                :, column * LANES : (column + 1) * LANES
            ].reshape(PLANE, rows, LANES)
    out[:, 3 * FHID // LANES * rows :, :] = jnp.broadcast_to(tag[None], (PLANE, 16, LANES))


def attention_kernel(place, first, side, edge_low, edge_high, out, earlier):
    span = first.shape[0] * TOK
    scale = 1.0 / math.sqrt(LANES)
    tile = 128
    reach = span + tile
    row = lax.broadcasted_iota(jnp.int32, (tile, reach), 0)
    col = lax.broadcasted_iota(jnp.int32, (tile, reach), 1)
    band = (col > row) & (col - row <= span)
    begin = jnp.where(place[0] == 0, span, 0)
    edge = lax.rem(place[0], YS) == 0
    heads = 2

    @pl.when(edge)
    def _():
        earlier[:, : 2 * TOK, :] = edge_low[...]
        earlier[:, 2 * TOK :, :] = edge_high[...]

    @pl.when(jnp.logical_not(edge))
    def _():
        earlier[...] = side[...]

    for head in range(heads):
        query = block_rows(first, 8 + head, 1)
        key = jnp.concatenate([block_rows(earlier, head, 1), block_rows(first, head, 1)], axis=0)
        value = jnp.concatenate(
            [block_rows(earlier, heads + head, 1), block_rows(first, heads + head, 1)], axis=0
        )
        for step in range(span // tile):
            low = step * tile
            scores = dot(query[low : low + tile], key[low : low + reach], ((1,), (1,))) * scale
            keep = band & (col + low >= begin)
            scores = jnp.where(keep, scores, -1e30)
            terms = jnp.exp(scores - jnp.max(scores, axis=1, keepdims=True))
            probs = (terms * (1.0 / jnp.sum(terms, axis=1, keepdims=True))).astype(jnp.bfloat16)
            out[pl.ds(low * heads + head, tile, stride=heads), :] = dot(
                probs, value[low : low + reach]
            )


def split(a):
    high = a.astype(jnp.bfloat16)
    return high, (a - high.astype(jnp.float32)).astype(jnp.bfloat16)


def orthogonal(ortho_all):
    for _ in range(NS_STEPS):
        grams, polys, nexts = [], [], []
        halves = [split(ortho) for ortho in ortho_all]
        for high, low in halves:
            cross = dot(high, low, ((1,), (1,)))
            grams.append(dot(high, high, ((1,), (1,))) + (cross + cross.T))
        for gram in grams:
            high, low = split(gram)
            square = dot(high, high) + (dot(high, low) + dot(low, high))
            polys.append(coef_b * gram + coef_c * square)
        for ortho, poly, (high, low) in zip(ortho_all, polys, halves):
            top, rest = split(poly)
            nexts.append(coef_a * ortho + (dot(top, high) + (dot(top, low) + dot(rest, high))))
        ortho_all = nexts
    return ortho_all


def apply_kernel(powers, every, gate, up, down, first, out):
    rows = FD // PLANE
    starts = []
    for matrix in range(3):
        columns = []
        for column in range(FHID // LANES):
            start = (matrix * (FHID // LANES) + column) * rows
            columns.append(every[:, start : start + rows, :].reshape(FD, LANES))
        total = jnp.concatenate(columns, axis=1)
        squares = jnp.sum(jnp.sum(total * total, axis=0, keepdims=True), axis=1, keepdims=True)
        factor = powers[matrix : matrix + 1, 0:1]
        starts.append(total * (factor / jnp.sqrt(squares * factor * factor + 1e-6)))
    ortho = orthogonal(starts)
    new_gate = (gate[...] + ortho[0]).astype(jnp.bfloat16)
    new_up = (up[...] + ortho[1]).astype(jnp.bfloat16)
    new_down = (down[...] + ortho[2].T).astype(jnp.bfloat16)
    query = block_rows(first, 10, 2)
    gate_pre = dot(query, new_gate)
    up_pre = dot(query, new_up)
    hidden = (gate_pre * (1.0 / (1.0 + jnp.exp(-gate_pre))) * up_pre).astype(jnp.bfloat16)
    result = dot(hidden, new_down)
    span = result.shape[0]
    for column in range(FD // LANES):
        out[pl.ds(column, span, stride=FD // LANES), :] = result[
            :, column * LANES : (column + 1) * LANES
        ]


def call(kernel, shape, operands, flops, scalars=0, scratch=()):
    vmem = pl.BlockSpec(memory_space=pltpu.VMEM)
    smem = pl.BlockSpec(memory_space=pltpu.SMEM)
    return pl.pallas_call(
        kernel,
        out_shape=jax.ShapeDtypeStruct(shape, jnp.float32),
        in_specs=[smem] * scalars + [vmem] * (len(operands) - scalars),
        out_specs=vmem,
        scratch_shapes=scratch,
        compiler_params=pltpu.CompilerParams(vmem_limit_bytes=VMEM_LIMIT),
        cost_estimate=pl.CostEstimate(flops=flops, bytes_accessed=4 << 20, transcendentals=0),
    )(*operands)


def wide_index(x, half, y):
    return (x * HALVES + half) * YS + y


PLANES = [[wide_index(x, half, y) for x in range(XS) for y in range(YS)] for half in range(HALVES)]
SWAP = [
    (wide_index(x, half, y), wide_index(x, 1 - half, y))
    for x in range(XS)
    for half in range(HALVES)
    for y in range(YS)
]
AROUND = [
    (wide_index(x, half, y), wide_index(x, half, (y + 1) % YS))
    for x in range(XS)
    for half in range(HALVES)
    for y in range(YS)
]
ENDS = [(x, half, x + half, 1 - half) for x in range(XS) for half in range(HALVES)][:-1]
EDGE_LOW = [(wide_index(x, half, 0), wide_index(*after, 0)) for x, half, *after in ENDS]
EDGE_HIGH = [(wide_index(x, half, YS - 1), wide_index(*after, 0)) for x, half, *after in ENDS]
FLOPS = 1 << 20


def tag_rows(power):
    wide = jnp.broadcast_to(power.astype(jnp.float16)[:, None], (3, LANES))
    return jnp.concatenate([wide, jnp.zeros((13, LANES), jnp.float16)], axis=0)


def per_device(query_key, value_heads, fast_inputs, rate_logits, gate_fast, up_fast, down_fast):
    group = lax.axis_size("narrow")
    rows = query_key.shape[0]
    own = query_key.shape[1] // group
    span = rows * group
    pair = query_key.reshape(rows, group, own, 2, LANES)
    query = pair[:, :, :, 0].transpose(1, 2, 0, 3)
    key = pair[:, :, :, 1].transpose(1, 2, 0, 3)
    value = value_heads.reshape(rows, group, own, LANES).transpose(1, 2, 0, 3)
    fast = fast_inputs.reshape(rows, group, 6, LANES).transpose(1, 2, 0, 3)
    logits = jnp.pad(rate_logits.transpose(1, 2, 0), ((0, 0), (0, 13), (0, LANES - rows)))
    blocks = jnp.concatenate([key, value, fast[:, 2:], query, fast[:, :2]], axis=1)
    blocks = blocks.reshape(group, 12 * rows, LANES)
    first = jnp.concatenate([blocks, logits], axis=1)
    first = lax.all_to_all(first, "narrow", 0, 0, tiled=True)
    tail = first[:, : 4 * rows]
    side = lax.ppermute(tail, "wide", AROUND)

    weights = (gate_fast[0], up_fast[0], down_fast[0])
    count = 3 * FHID // LANES * FD // PLANE
    pieces = call(gradient_kernel, (PLANE, count + 16, LANES), (first, *weights), FLOPS)
    got = lax.all_to_all(
        pieces.astype(jnp.float16), "wide", 0, 0, tiled=True, axis_index_groups=PLANES
    )
    got, side = lax.optimization_barrier((got, side))
    powers = got[:, count : count + 3, 0].astype(jnp.float32)
    top = jnp.max(powers, axis=0)
    parts = got[:, :count].astype(jnp.float32).reshape(PLANE, 3, -1, LANES)
    half = jnp.sum(parts * (jnp.exp2(powers - top) * 0.0625)[:, :, None, None], axis=0)
    sent = jnp.concatenate([half.astype(jnp.float16).reshape(count, LANES), tag_rows(top)], axis=0)
    other = lax.ppermute(sent, "wide", SWAP)
    other, low_part, high_part = lax.optimization_barrier(
        (other, side[:, : 2 * rows], tail[:, 2 * rows :])
    )
    edge_low = lax.ppermute(low_part, "wide", EDGE_LOW)
    edge_high = lax.ppermute(high_part, "wide", EDGE_HIGH)
    other_top = other[count : count + 3, 0].astype(jnp.float32)
    both = jnp.maximum(top, other_top)
    whole = half * (jnp.exp2(top - both) * 0.5)[:, None, None]
    whole = whole + other[:count].astype(jnp.float32).reshape(3, -1, LANES) * (
        jnp.exp2(other_top - both) * 0.5
    )[:, None, None]
    whole = whole.astype(jnp.float16).reshape(count, LANES)
    every = lax.all_to_all(
        jnp.broadcast_to(whole[None], (PLANE, count, LANES)),
        "wide",
        0,
        0,
        tiled=True,
        axis_index_groups=PLANES,
    )
    factors = jnp.broadcast_to(
        jnp.concatenate([jnp.exp2(both - 8.0), jnp.zeros((5,), jnp.float32)])[:, None], (8, LANES)
    )
    fast_out = call(
        apply_kernel,
        (span * FD // LANES, LANES),
        (factors, every.astype(jnp.float32), *weights, first),
        FLOPS,
    )
    place = lax.axis_index("wide").reshape(1)
    edge_low, edge_high, fast_out = lax.optimization_barrier((edge_low, edge_high, fast_out))
    window_out = call(
        attention_kernel,
        (span * own, LANES),
        (place, first, side, edge_low, edge_high),
        FLOPS,
        1,
        [pltpu.VMEM((PLANE, 4 * TOK, LANES), jnp.bfloat16)],
    )
    return (window_out.reshape(span, own, LANES), fast_out.reshape(span, 1, FD))


def solution(mesh):
    return jax.shard_map(
        per_device,
        mesh=mesh,
        in_specs=(
            P(("wide", "narrow"), None, None),
            P(("wide", "narrow"), None, None),
            P(("wide", "narrow"), None, None),
            P(("wide", "narrow"), None, None),
            P("narrow", None, None),
            P("narrow", None, None),
            P("narrow", None, None),
        ),
        out_specs=(P("wide", "narrow", None), P("wide", "narrow", None)),
        check_vma=False,
    )
```

```python
import math

import jax
import jax.numpy as jnp
from jax import lax
from jax.experimental import pallas as pl
from jax.experimental.pallas import tpu as pltpu
from jax.sharding import PartitionSpec as P

FD = 256
FHID = 512
WINDOW = 512
NS_STEPS = 5
LANES = 128
TOK = 32

coef_a = 3.4445
coef_b = -4.775
coef_c = 2.0315

XS, HALVES, YS = 4, 2, 4
PLANE = XS * YS
VMEM_LIMIT = 48 * 1024 * 1024


def dot(a, b, dims=((1,), (0,))):
    return lax.dot_general(a, b, (dims, ((), ())), preferred_element_type=jnp.float32)


def block_rows(ref, index, count):
    group = ref.shape[0]
    parts = [
        ref[:, (index + i) * TOK : (index + i + 1) * TOK, :].reshape(group * TOK, LANES)
        for i in range(count)
    ]
    return parts[0] if count == 1 else jnp.concatenate(parts, axis=1)


def gradient_kernel(first, gate, up, down, out):
    group = first.shape[0]
    span = group * TOK
    logits = first[:, 12 * TOK : 12 * TOK + 16, :].astype(jnp.float32)
    rate_blocks = []
    for source in range(group):
        turned = logits[source].T[:TOK]
        rate_blocks.append(jnp.maximum(turned, 0.0) + jnp.log1p(jnp.exp(-jnp.abs(turned))))
    rates = jnp.concatenate(rate_blocks, axis=0)
    key = block_rows(first, 4, 2)
    value = block_rows(first, 6, 2)
    gate_bf = gate[...].astype(jnp.bfloat16)
    up_bf = up[...].astype(jnp.bfloat16)
    down_bf = down[...].astype(jnp.bfloat16)
    totals = [None, None, None]
    half = span // 2
    for part in range(2):
        rows = slice(part * half, (part + 1) * half)
        key_part, value_part, rate = key[rows], value[rows], rates[rows]
        gate_pre = dot(key_part, gate_bf)
        up_pre = dot(key_part, up_bf)
        back = dot(value_part, down_bf, ((1,), (1,)))
        sigmoid_gate = 1.0 / (1.0 + jnp.exp(-gate_pre))
        activated = gate_pre * sigmoid_gate
        hidden = (activated * up_pre).astype(jnp.bfloat16)
        scaled_v = (rate[:, 1:2] * value_part.astype(jnp.float32)).astype(jnp.bfloat16)
        grad_gate = (
            rate[:, 0:1] * back * up_pre * sigmoid_gate * (1.0 + gate_pre * (1.0 - sigmoid_gate))
        ).astype(jnp.bfloat16)
        grad_up = (rate[:, 2:3] * back * activated).astype(jnp.bfloat16)
        fresh = (
            dot(key_part, grad_gate, ((0,), (0,))),
            dot(key_part, grad_up, ((0,), (0,))),
            dot(scaled_v, hidden, ((0,), (0,))),
        )
        totals = [new if old is None else old + new for old, new in zip(totals, fresh)]
    rows = FD // PLANE
    row = lax.broadcasted_iota(jnp.int32, (16, LANES), 0)
    tag = jnp.zeros((16, LANES), jnp.float32)
    for matrix, total in enumerate(totals):
        most = jnp.max(jnp.max(jnp.abs(total), axis=0, keepdims=True), axis=1, keepdims=True)
        power = jnp.floor(jnp.log(jnp.maximum(most, 1e-30)) * 1.4426950408889634)
        scaled = total * jnp.exp((13.0 - power) * 0.6931471805599453)
        tag = jnp.where(row == matrix, power, tag)
        for column in range(FHID // LANES):
            start = (matrix * (FHID // LANES) + column) * rows
            out[:, start : start + rows, :] = scaled[
                :, column * LANES : (column + 1) * LANES
            ].reshape(PLANE, rows, LANES)
    out[:, 3 * FHID // LANES * rows :, :] = jnp.broadcast_to(tag[None], (PLANE, 16, LANES))


def attention_kernel(place, first, side, edge_low, edge_high, out, earlier):
    span = first.shape[0] * TOK
    scale = 1.0 / math.sqrt(LANES)
    tile = 128
    reach = span + tile
    row = lax.broadcasted_iota(jnp.int32, (tile, reach), 0)
    col = lax.broadcasted_iota(jnp.int32, (tile, reach), 1)
    band = (col > row) & (col - row <= span)
    begin = jnp.where(place[0] == 0, span, 0)
    edge = lax.rem(place[0], YS) == 0
    heads = 2

    @pl.when(edge)
    def _():
        earlier[:, : 2 * TOK, :] = edge_low[...]
        earlier[:, 2 * TOK :, :] = edge_high[...]

    @pl.when(jnp.logical_not(edge))
    def _():
        earlier[...] = side[...]

    for head in range(heads):
        query = block_rows(first, 8 + head, 1)
        key = jnp.concatenate([block_rows(earlier, head, 1), block_rows(first, head, 1)], axis=0)
        value = jnp.concatenate(
            [block_rows(earlier, heads + head, 1), block_rows(first, heads + head, 1)], axis=0
        )
        for step in range(span // tile):
            low = step * tile
            scores = dot(query[low : low + tile], key[low : low + reach], ((1,), (1,))) * scale
            keep = band & (col + low >= begin)
            scores = jnp.where(keep, scores, -1e30)
            terms = jnp.exp(scores - jnp.max(scores, axis=1, keepdims=True))
            probs = (terms * (1.0 / jnp.sum(terms, axis=1, keepdims=True))).astype(jnp.bfloat16)
            out[pl.ds(low * heads + head, tile, stride=heads), :] = dot(
                probs, value[low : low + reach]
            )


def split(a):
    high = a.astype(jnp.bfloat16)
    return high, (a - high.astype(jnp.float32)).astype(jnp.bfloat16)


def orthogonal(ortho_all):
    for _ in range(NS_STEPS):
        grams, polys, nexts = [], [], []
        halves = [split(ortho) for ortho in ortho_all]
        for high, low in halves:
            cross = dot(high, low, ((1,), (1,)))
            grams.append(dot(high, high, ((1,), (1,))) + (cross + cross.T))
        for gram in grams:
            high, low = split(gram)
            square = dot(high, high) + (dot(high, low) + dot(low, high))
            polys.append(coef_b * gram + coef_c * square)
        for ortho, poly, (high, low) in zip(ortho_all, polys, halves):
            top, rest = split(poly)
            nexts.append(coef_a * ortho + (dot(top, high) + (dot(top, low) + dot(rest, high))))
        ortho_all = nexts
    return ortho_all


def apply_kernel(powers, every, gate, up, down, first, out):
    rows = FD // PLANE
    starts = []
    for matrix in range(3):
        columns = []
        for column in range(FHID // LANES):
            start = (matrix * (FHID // LANES) + column) * rows
            columns.append(every[:, start : start + rows, :].reshape(FD, LANES))
        total = jnp.concatenate(columns, axis=1)
        squares = jnp.sum(jnp.sum(total * total, axis=0, keepdims=True), axis=1, keepdims=True)
        factor = powers[matrix : matrix + 1, 0:1]
        starts.append(total * (factor / jnp.sqrt(squares * factor * factor + 1e-6)))
    ortho = orthogonal(starts)
    new_gate = (gate[...] + ortho[0]).astype(jnp.bfloat16)
    new_up = (up[...] + ortho[1]).astype(jnp.bfloat16)
    new_down = (down[...] + ortho[2].T).astype(jnp.bfloat16)
    query = block_rows(first, 10, 2)
    gate_pre = dot(query, new_gate)
    up_pre = dot(query, new_up)
    hidden = (gate_pre * (1.0 / (1.0 + jnp.exp(-gate_pre))) * up_pre).astype(jnp.bfloat16)
    result = dot(hidden, new_down)
    span = result.shape[0]
    for column in range(FD // LANES):
        out[pl.ds(column, span, stride=FD // LANES), :] = result[
            :, column * LANES : (column + 1) * LANES
        ]


def call(kernel, shape, operands, flops, scalars=0, scratch=()):
    vmem = pl.BlockSpec(memory_space=pltpu.VMEM)
    smem = pl.BlockSpec(memory_space=pltpu.SMEM)
    return pl.pallas_call(
        kernel,
        out_shape=jax.ShapeDtypeStruct(shape, jnp.float32),
        in_specs=[smem] * scalars + [vmem] * (len(operands) - scalars),
        out_specs=vmem,
        scratch_shapes=scratch,
        compiler_params=pltpu.CompilerParams(vmem_limit_bytes=VMEM_LIMIT),
        cost_estimate=pl.CostEstimate(flops=flops, bytes_accessed=4 << 20, transcendentals=0),
    )(*operands)


def wide_index(x, half, y):
    return (x * HALVES + half) * YS + y


PLANES = [[wide_index(x, half, y) for x in range(XS) for y in range(YS)] for half in range(HALVES)]
SWAP = [
    (wide_index(x, half, y), wide_index(x, 1 - half, y))
    for x in range(XS)
    for half in range(HALVES)
    for y in range(YS)
]
AROUND = [
    (wide_index(x, half, y), wide_index(x, half, (y + 1) % YS))
    for x in range(XS)
    for half in range(HALVES)
    for y in range(YS)
]
ENDS = [(x, half, x + half, 1 - half) for x in range(XS) for half in range(HALVES)][:-1]
EDGE_LOW = [(wide_index(x, half, 0), wide_index(*after, 0)) for x, half, *after in ENDS]
EDGE_HIGH = [(wide_index(x, half, YS - 1), wide_index(*after, 0)) for x, half, *after in ENDS]
FLOPS = 1 << 20


def per_device(query_key, value_heads, fast_inputs, rate_logits, gate_fast, up_fast, down_fast):
    group = lax.axis_size("narrow")
    rows = query_key.shape[0]
    own = query_key.shape[1] // group
    span = rows * group
    pair = query_key.transpose(1, 0, 2).reshape(group, own * rows, 2 * LANES)
    value = value_heads.transpose(1, 0, 2).reshape(group, own * rows, LANES)
    fast = fast_inputs.transpose(1, 0, 2)
    fast = [fast[:, :, i * LANES : (i + 1) * LANES] for i in range(6)]
    logits = jnp.pad(rate_logits.transpose(1, 2, 0), ((0, 0), (0, 13), (0, LANES - rows)))
    first = jnp.concatenate(
        [pair[:, :, LANES:], value, *fast[2:], pair[:, :, :LANES], *fast[:2], logits], axis=1
    )
    first = lax.all_to_all(first, "narrow", 0, 0, tiled=True)
    tail = first[:, : 4 * rows]

    weights = (gate_fast[0], up_fast[0], down_fast[0])
    count = 3 * FHID // LANES * FD // PLANE
    pieces = call(gradient_kernel, (PLANE, count + 16, LANES), (first, *weights), FLOPS)
    got = lax.all_to_all(
        pieces.astype(jnp.float16), "wide", 0, 0, tiled=True, axis_index_groups=PLANES
    )
    got, tail = lax.optimization_barrier((got, tail))
    side = lax.ppermute(tail, "wide", AROUND)
    powers = got[:, count : count + 3].astype(jnp.float32)
    top = jnp.max(powers, axis=0)
    parts = got[:, :count].astype(jnp.float32).reshape(PLANE, 3, -1, LANES)
    half = jnp.sum(parts * (jnp.exp2(powers - top) * 0.0625)[:, :, None], axis=0)
    sent = jnp.concatenate(
        [half.reshape(count, LANES), top, jnp.zeros((13, LANES), jnp.float32)], axis=0
    )
    sent = sent.astype(jnp.float16)
    other = lax.ppermute(sent, "wide", SWAP)
    other, low_part, high_part = lax.optimization_barrier(
        (other, side[:, : 2 * rows], tail[:, 2 * rows :])
    )
    edge_low = lax.ppermute(low_part, "wide", EDGE_LOW)
    edge_high = lax.ppermute(high_part, "wide", EDGE_HIGH)
    other_top = other[count : count + 3].astype(jnp.float32)
    both = jnp.maximum(top, other_top)
    whole = half * (jnp.exp2(top - both) * 0.5)[:, None]
    whole = whole + other[:count].astype(jnp.float32).reshape(3, -1, LANES) * (
        jnp.exp2(other_top - both) * 0.5
    )[:, None]
    whole = whole.astype(jnp.float16).reshape(count, LANES)
    every = lax.all_to_all(
        jnp.broadcast_to(whole[None], (PLANE, count, LANES)),
        "wide",
        0,
        0,
        tiled=True,
        axis_index_groups=PLANES,
    )
    factors = jnp.concatenate([jnp.exp2(both - 8.0), jnp.zeros((5, LANES), jnp.float32)], axis=0)
    fast_out = call(
        apply_kernel,
        (span * FD // LANES, LANES),
        (factors, every.astype(jnp.float32), *weights, first),
        FLOPS,
    )
    place = lax.axis_index("wide").reshape(1)
    edge_low, edge_high, fast_out = lax.optimization_barrier((edge_low, edge_high, fast_out))
    window_out = call(
        attention_kernel,
        (span * own, LANES),
        (place, first, side, edge_low, edge_high),
        FLOPS,
        1,
        [pltpu.VMEM((PLANE, 4 * TOK, LANES), jnp.bfloat16)],
    )
    return (window_out.reshape(span, own, LANES), fast_out.reshape(span, 1, FD))


def solution(mesh):
    return jax.shard_map(
        per_device,
        mesh=mesh,
        in_specs=(
            P(("wide", "narrow"), None, None),
            P(("wide", "narrow"), None, None),
            P(("wide", "narrow"), None, None),
            P(("wide", "narrow"), None, None),
            P("narrow", None, None),
            P("narrow", None, None),
            P("narrow", None, None),
        ),
        out_specs=(P("wide", "narrow", None), P("wide", "narrow", None)),
        check_vma=False,
    )
```

```python
import math

import jax
import jax.numpy as jnp
from jax import lax
from jax.experimental import pallas as pl
from jax.experimental.pallas import tpu as pltpu
from jax.sharding import PartitionSpec as P

FD = 256
FHID = 512
WINDOW = 512
NS_STEPS = 5
LANES = 128
TOK = 32

coef_a = 3.4445
coef_b = -4.775
coef_c = 2.0315

XS, HALVES, YS = 4, 2, 4
PLANE = XS * YS
VMEM_LIMIT = 48 * 1024 * 1024


def dot(a, b, dims=((1,), (0,))):
    return lax.dot_general(a, b, (dims, ((), ())), preferred_element_type=jnp.float32)


def block_rows(ref, index, count):
    group = ref.shape[0]
    parts = [
        ref[:, (index + i) * TOK : (index + i + 1) * TOK, :].reshape(group * TOK, LANES)
        for i in range(count)
    ]
    return parts[0] if count == 1 else jnp.concatenate(parts, axis=1)


def gradient_kernel(first, gate, up, down, out):
    group = first.shape[0]
    span = group * TOK
    logits = first[:, 12 * TOK : 12 * TOK + 16, :].astype(jnp.float32)
    rate_blocks = []
    for source in range(group):
        turned = logits[source].T[:TOK]
        rate_blocks.append(jnp.maximum(turned, 0.0) + jnp.log1p(jnp.exp(-jnp.abs(turned))))
    rates = jnp.concatenate(rate_blocks, axis=0)
    key = block_rows(first, 4, 2)
    value = block_rows(first, 6, 2)
    gate_bf = gate[...].astype(jnp.bfloat16)
    up_bf = up[...].astype(jnp.bfloat16)
    down_bf = down[...].astype(jnp.bfloat16)
    totals = [None, None, None]
    half = span // 2
    for part in range(2):
        rows = slice(part * half, (part + 1) * half)
        key_part, value_part, rate = key[rows], value[rows], rates[rows]
        gate_pre = dot(key_part, gate_bf)
        up_pre = dot(key_part, up_bf)
        back = dot(value_part, down_bf, ((1,), (1,)))
        sigmoid_gate = 1.0 / (1.0 + jnp.exp(-gate_pre))
        activated = gate_pre * sigmoid_gate
        hidden = (activated * up_pre).astype(jnp.bfloat16)
        scaled_v = (rate[:, 1:2] * value_part.astype(jnp.float32)).astype(jnp.bfloat16)
        grad_gate = (
            rate[:, 0:1] * back * up_pre * sigmoid_gate * (1.0 + gate_pre * (1.0 - sigmoid_gate))
        ).astype(jnp.bfloat16)
        grad_up = (rate[:, 2:3] * back * activated).astype(jnp.bfloat16)
        fresh = (
            dot(key_part, grad_gate, ((0,), (0,))),
            dot(key_part, grad_up, ((0,), (0,))),
            dot(scaled_v, hidden, ((0,), (0,))),
        )
        totals = [new if old is None else old + new for old, new in zip(totals, fresh)]
    rows = FD // PLANE
    row = lax.broadcasted_iota(jnp.int32, (16, LANES), 0)
    tag = jnp.zeros((16, LANES), jnp.float32)
    for matrix, total in enumerate(totals):
        most = jnp.max(jnp.max(jnp.abs(total), axis=0, keepdims=True), axis=1, keepdims=True)
        power = jnp.floor(jnp.log(jnp.maximum(most, 1e-30)) * 1.4426950408889634)
        scaled = total * jnp.exp((13.0 - power) * 0.6931471805599453)
        tag = jnp.where(row == matrix, power, tag)
        for column in range(FHID // LANES):
            start = (matrix * (FHID // LANES) + column) * rows
            out[:, start : start + rows, :] = scaled[
                :, column * LANES : (column + 1) * LANES
            ].reshape(PLANE, rows, LANES)
    out[:, 3 * FHID // LANES * rows :, :] = jnp.broadcast_to(tag[None], (PLANE, 16, LANES))


def attention_kernel(place, first, side, edge_low, edge_high, out, earlier):
    span = first.shape[0] * TOK
    scale = 1.0 / math.sqrt(LANES)
    tile = 128
    reach = span + tile
    row = lax.broadcasted_iota(jnp.int32, (tile, reach), 0)
    col = lax.broadcasted_iota(jnp.int32, (tile, reach), 1)
    band = (col > row) & (col - row <= span)
    begin = jnp.where(place[0] == 0, span, 0)
    edge = lax.rem(place[0], YS) == 0
    heads = 2

    @pl.when(edge)
    def _():
        earlier[:, : 2 * TOK, :] = edge_low[...]
        earlier[:, 2 * TOK :, :] = edge_high[...]

    @pl.when(jnp.logical_not(edge))
    def _():
        earlier[...] = side[...]

    for head in range(heads):
        query = block_rows(first, 8 + head, 1)
        key = jnp.concatenate([block_rows(earlier, head, 1), block_rows(first, head, 1)], axis=0)
        value = jnp.concatenate(
            [block_rows(earlier, heads + head, 1), block_rows(first, heads + head, 1)], axis=0
        )
        for step in range(span // tile):
            low = step * tile
            scores = dot(query[low : low + tile], key[low : low + reach], ((1,), (1,))) * scale
            keep = band & (col + low >= begin)
            scores = jnp.where(keep, scores, -1e30)
            terms = jnp.exp(scores - jnp.max(scores, axis=1, keepdims=True))
            probs = (terms * (1.0 / jnp.sum(terms, axis=1, keepdims=True))).astype(jnp.bfloat16)
            out[pl.ds(low * heads + head, tile, stride=heads), :] = dot(
                probs, value[low : low + reach]
            )


def split(a):
    high = a.astype(jnp.bfloat16)
    return high, (a - high.astype(jnp.float32)).astype(jnp.bfloat16)


def orthogonal(ortho_all):
    for _ in range(NS_STEPS):
        grams, polys, nexts = [], [], []
        halves = [split(ortho) for ortho in ortho_all]
        for high, low in halves:
            cross = dot(high, low, ((1,), (1,)))
            grams.append(dot(high, high, ((1,), (1,))) + (cross + cross.T))
        for gram in grams:
            high, low = split(gram)
            square = dot(high, high) + (dot(high, low) + dot(low, high))
            polys.append(coef_b * gram + coef_c * square)
        for ortho, poly, (high, low) in zip(ortho_all, polys, halves):
            top, rest = split(poly)
            nexts.append(coef_a * ortho + (dot(top, high) + (dot(top, low) + dot(rest, high))))
        ortho_all = nexts
    return ortho_all


def apply_kernel(powers, every, gate, up, down, first, out):
    rows = FD // PLANE
    starts = []
    for matrix in range(3):
        columns = []
        for column in range(FHID // LANES):
            start = (matrix * (FHID // LANES) + column) * rows
            columns.append(every[:, start : start + rows, :].reshape(FD, LANES))
        total = jnp.concatenate(columns, axis=1)
        squares = jnp.sum(jnp.sum(total * total, axis=0, keepdims=True), axis=1, keepdims=True)
        factor = powers[matrix : matrix + 1, 0:1]
        starts.append(total * (factor / jnp.sqrt(squares * factor * factor + 1e-6)))
    ortho = orthogonal(starts)
    new_gate = (gate[...] + ortho[0]).astype(jnp.bfloat16)
    new_up = (up[...] + ortho[1]).astype(jnp.bfloat16)
    new_down = (down[...] + ortho[2].T).astype(jnp.bfloat16)
    query = block_rows(first, 10, 2)
    gate_pre = dot(query, new_gate)
    up_pre = dot(query, new_up)
    hidden = (gate_pre * (1.0 / (1.0 + jnp.exp(-gate_pre))) * up_pre).astype(jnp.bfloat16)
    result = dot(hidden, new_down)
    span = result.shape[0]
    for column in range(FD // LANES):
        out[pl.ds(column, span, stride=FD // LANES), :] = result[
            :, column * LANES : (column + 1) * LANES
        ]


def call(kernel, shape, operands, flops, scalars=0, scratch=()):
    vmem = pl.BlockSpec(memory_space=pltpu.VMEM)
    smem = pl.BlockSpec(memory_space=pltpu.SMEM)
    return pl.pallas_call(
        kernel,
        out_shape=jax.ShapeDtypeStruct(shape, jnp.float32),
        in_specs=[smem] * scalars + [vmem] * (len(operands) - scalars),
        out_specs=vmem,
        scratch_shapes=scratch,
        compiler_params=pltpu.CompilerParams(vmem_limit_bytes=VMEM_LIMIT),
        cost_estimate=pl.CostEstimate(flops=flops, bytes_accessed=4 << 20, transcendentals=0),
    )(*operands)


def wide_index(x, half, y):
    return (x * HALVES + half) * YS + y


PLANES = [[wide_index(x, half, y) for x in range(XS) for y in range(YS)] for half in range(HALVES)]
SWAP = [
    (wide_index(x, half, y), wide_index(x, 1 - half, y))
    for x in range(XS)
    for half in range(HALVES)
    for y in range(YS)
]
AROUND = [
    (wide_index(x, half, y), wide_index(x, half, (y + 1) % YS))
    for x in range(XS)
    for half in range(HALVES)
    for y in range(YS)
]
ENDS = [(x, half, x + half, 1 - half) for x in range(XS) for half in range(HALVES)][:-1]
EDGE_LOW = [(wide_index(x, half, 0), wide_index(*after, 0)) for x, half, *after in ENDS]
EDGE_HIGH = [(wide_index(x, half, YS - 1), wide_index(*after, 0)) for x, half, *after in ENDS]
FLOPS = 1 << 20


def per_device(query_key, value_heads, fast_inputs, rate_logits, gate_fast, up_fast, down_fast):
    group = lax.axis_size("narrow")
    rows = query_key.shape[0]
    own = query_key.shape[1] // group
    span = rows * group
    pair = query_key.transpose(1, 0, 2).reshape(group, own * rows, 2 * LANES)
    value = value_heads.transpose(1, 0, 2).reshape(group, own * rows, LANES)
    fast = fast_inputs.transpose(1, 0, 2)
    fast = [fast[:, :, i * LANES : (i + 1) * LANES] for i in range(6)]
    logits = jnp.pad(rate_logits.transpose(1, 2, 0), ((0, 0), (0, 13), (0, LANES - rows)))
    first = jnp.concatenate(
        [pair[:, :, LANES:], value, *fast[2:], pair[:, :, :LANES], *fast[:2], logits], axis=1
    )
    first = lax.all_to_all(first, "narrow", 0, 0, tiled=True)
    tail = first[:, : 4 * rows]
    edge_high = lax.ppermute(first[:, 2 * rows : 4 * rows], "wide", EDGE_HIGH)

    weights = (gate_fast[0], up_fast[0], down_fast[0])
    count = 3 * FHID // LANES * FD // PLANE
    pieces = call(gradient_kernel, (PLANE, count + 16, LANES), (first, *weights), FLOPS)
    got = lax.all_to_all(
        pieces.astype(jnp.float16), "wide", 0, 0, tiled=True, axis_index_groups=PLANES
    )
    got, tail = lax.optimization_barrier((got, tail))
    side = lax.ppermute(tail, "wide", AROUND)
    powers = got[:, count : count + 3].astype(jnp.float32)
    top = jnp.max(powers, axis=0)
    parts = got[:, :count].astype(jnp.float32).reshape(PLANE, 3, -1, LANES)
    half = jnp.sum(parts * (jnp.exp2(powers - top) * 0.0625)[:, :, None], axis=0)
    sent = jnp.concatenate(
        [half.reshape(count, LANES), top, jnp.zeros((13, LANES), jnp.float32)], axis=0
    )
    sent = sent.astype(jnp.float16)
    other = lax.ppermute(sent, "wide", SWAP)
    other, low_part, edge_high = lax.optimization_barrier((other, side[:, : 2 * rows], edge_high))
    edge_low = lax.ppermute(low_part, "wide", EDGE_LOW)
    other_top = other[count : count + 3].astype(jnp.float32)
    both = jnp.maximum(top, other_top)
    whole = half * (jnp.exp2(top - both) * 0.5)[:, None]
    whole = whole + other[:count].astype(jnp.float32).reshape(3, -1, LANES) * (
        jnp.exp2(other_top - both) * 0.5
    )[:, None]
    whole = whole.astype(jnp.float16).reshape(count, LANES)
    every = lax.all_to_all(
        jnp.broadcast_to(whole[None], (PLANE, count, LANES)),
        "wide",
        0,
        0,
        tiled=True,
        axis_index_groups=PLANES,
    )
    factors = jnp.concatenate([jnp.exp2(both - 8.0), jnp.zeros((5, LANES), jnp.float32)], axis=0)
    fast_out = call(
        apply_kernel,
        (span * FD // LANES, LANES),
        (factors, every.astype(jnp.float32), *weights, first),
        FLOPS,
    )
    place = lax.axis_index("wide").reshape(1)
    edge_low, fast_out = lax.optimization_barrier((edge_low, fast_out))
    window_out = call(
        attention_kernel,
        (span * own, LANES),
        (place, first, side, edge_low, edge_high),
        FLOPS,
        1,
        [pltpu.VMEM((PLANE, 4 * TOK, LANES), jnp.bfloat16)],
    )
    return (window_out.reshape(span, own, LANES), fast_out.reshape(span, 1, FD))


def solution(mesh):
    return jax.shard_map(
        per_device,
        mesh=mesh,
        in_specs=(
            P(("wide", "narrow"), None, None),
            P(("wide", "narrow"), None, None),
            P(("wide", "narrow"), None, None),
            P(("wide", "narrow"), None, None),
            P("narrow", None, None),
            P("narrow", None, None),
            P("narrow", None, None),
        ),
        out_specs=(P("wide", "narrow", None), P("wide", "narrow", None)),
        check_vma=False,
    )
```

```python
import math

import jax
import jax.numpy as jnp
from jax import lax
from jax.experimental import pallas as pl
from jax.experimental.pallas import tpu as pltpu
from jax.sharding import PartitionSpec as P

FD = 256
FHID = 512
WINDOW = 512
NS_STEPS = 5
LANES = 128
TOK = 32

coef_a = 3.4445
coef_b = -4.775
coef_c = 2.0315

XS, HALVES, YS = 4, 2, 4
PLANE = XS * YS
VMEM_LIMIT = 48 * 1024 * 1024


def dot(a, b, dims=((1,), (0,))):
    return lax.dot_general(a, b, (dims, ((), ())), preferred_element_type=jnp.float32)


def block_rows(ref, index, count):
    group = ref.shape[0]
    parts = [
        ref[:, (index + i) * TOK : (index + i + 1) * TOK, :].reshape(group * TOK, LANES)
        for i in range(count)
    ]
    return parts[0] if count == 1 else jnp.concatenate(parts, axis=1)


def gradient_kernel(first, gate, up, down, out):
    group = first.shape[0]
    span = group * TOK
    logits = first[:, 8 * TOK : 8 * TOK + 16, :].astype(jnp.float32)
    rate_blocks = []
    for source in range(group):
        turned = logits[source].T[:TOK]
        rate_blocks.append(jnp.maximum(turned, 0.0) + jnp.log1p(jnp.exp(-jnp.abs(turned))))
    rates = jnp.concatenate(rate_blocks, axis=0)
    key = block_rows(first, 4, 2)
    value = block_rows(first, 6, 2)
    gate_bf = gate[...].astype(jnp.bfloat16)
    up_bf = up[...].astype(jnp.bfloat16)
    down_bf = down[...].astype(jnp.bfloat16)
    totals = [None, None, None]
    half = span // 2
    for part in range(2):
        rows = slice(part * half, (part + 1) * half)
        key_part, value_part, rate = key[rows], value[rows], rates[rows]
        gate_pre = dot(key_part, gate_bf)
        up_pre = dot(key_part, up_bf)
        back = dot(value_part, down_bf, ((1,), (1,)))
        sigmoid_gate = 1.0 / (1.0 + jnp.exp(-gate_pre))
        activated = gate_pre * sigmoid_gate
        hidden = (activated * up_pre).astype(jnp.bfloat16)
        scaled_v = (rate[:, 1:2] * value_part.astype(jnp.float32)).astype(jnp.bfloat16)
        grad_gate = (
            rate[:, 0:1] * back * up_pre * sigmoid_gate * (1.0 + gate_pre * (1.0 - sigmoid_gate))
        ).astype(jnp.bfloat16)
        grad_up = (rate[:, 2:3] * back * activated).astype(jnp.bfloat16)
        fresh = (
            dot(key_part, grad_gate, ((0,), (0,))),
            dot(key_part, grad_up, ((0,), (0,))),
            dot(scaled_v, hidden, ((0,), (0,))),
        )
        totals = [new if old is None else old + new for old, new in zip(totals, fresh)]
    rows = FD // PLANE
    row = lax.broadcasted_iota(jnp.int32, (16, LANES), 0)
    tag = jnp.zeros((16, LANES), jnp.float32)
    for matrix, total in enumerate(totals):
        most = jnp.max(jnp.max(jnp.abs(total), axis=0, keepdims=True), axis=1, keepdims=True)
        power = jnp.floor(jnp.log(jnp.maximum(most, 1e-30)) * 1.4426950408889634)
        scaled = total * jnp.exp((13.0 - power) * 0.6931471805599453)
        tag = jnp.where(row == matrix, power, tag)
        for column in range(FHID // LANES):
            start = (matrix * (FHID // LANES) + column) * rows
            out[:, start : start + rows, :] = scaled[
                :, column * LANES : (column + 1) * LANES
            ].reshape(PLANE, rows, LANES)
    out[:, 3 * FHID // LANES * rows :, :] = jnp.broadcast_to(tag[None], (PLANE, 16, LANES))


def attention_kernel(place, first, second, side, edge_low, edge_high, out, earlier):
    span = first.shape[0] * TOK
    scale = 1.0 / math.sqrt(LANES)
    tile = 128
    reach = span + tile
    row = lax.broadcasted_iota(jnp.int32, (tile, reach), 0)
    col = lax.broadcasted_iota(jnp.int32, (tile, reach), 1)
    band = (col > row) & (col - row <= span)
    begin = jnp.where(place[0] == 0, span, 0)
    edge = lax.rem(place[0], YS) == 0
    heads = 2

    @pl.when(edge)
    def _():
        earlier[:, : 2 * TOK, :] = edge_low[...]
        earlier[:, 2 * TOK :, :] = edge_high[...]

    @pl.when(jnp.logical_not(edge))
    def _():
        earlier[...] = side[...]

    for head in range(heads):
        query = block_rows(second, head, 1)
        key = jnp.concatenate([block_rows(earlier, head, 1), block_rows(first, head, 1)], axis=0)
        value = jnp.concatenate(
            [block_rows(earlier, heads + head, 1), block_rows(first, heads + head, 1)], axis=0
        )
        for step in range(span // tile):
            low = step * tile
            scores = dot(query[low : low + tile], key[low : low + reach], ((1,), (1,))) * scale
            keep = band & (col + low >= begin)
            scores = jnp.where(keep, scores, -1e30)
            terms = jnp.exp(scores - jnp.max(scores, axis=1, keepdims=True))
            probs = (terms * (1.0 / jnp.sum(terms, axis=1, keepdims=True))).astype(jnp.bfloat16)
            out[pl.ds(low * heads + head, tile, stride=heads), :] = dot(
                probs, value[low : low + reach]
            )


def split(a):
    high = a.astype(jnp.bfloat16)
    return high, (a - high.astype(jnp.float32)).astype(jnp.bfloat16)


def orthogonal(ortho_all):
    for _ in range(NS_STEPS):
        grams, polys, nexts = [], [], []
        halves = [split(ortho) for ortho in ortho_all]
        for high, low in halves:
            cross = dot(high, low, ((1,), (1,)))
            grams.append(dot(high, high, ((1,), (1,))) + (cross + cross.T))
        for gram in grams:
            high, low = split(gram)
            square = dot(high, high) + (dot(high, low) + dot(low, high))
            polys.append(coef_b * gram + coef_c * square)
        for ortho, poly, (high, low) in zip(ortho_all, polys, halves):
            top, rest = split(poly)
            nexts.append(coef_a * ortho + (dot(top, high) + (dot(top, low) + dot(rest, high))))
        ortho_all = nexts
    return ortho_all


def apply_kernel(powers, every, gate, up, down, second, out):
    rows = FD // PLANE
    starts = []
    for matrix in range(3):
        columns = []
        for column in range(FHID // LANES):
            start = (matrix * (FHID // LANES) + column) * rows
            columns.append(every[:, start : start + rows, :].reshape(FD, LANES))
        total = jnp.concatenate(columns, axis=1)
        squares = jnp.sum(jnp.sum(total * total, axis=0, keepdims=True), axis=1, keepdims=True)
        factor = powers[matrix : matrix + 1, 0:1]
        starts.append(total * (factor / jnp.sqrt(squares * factor * factor + 1e-6)))
    ortho = orthogonal(starts)
    new_gate = (gate[...] + ortho[0]).astype(jnp.bfloat16)
    new_up = (up[...] + ortho[1]).astype(jnp.bfloat16)
    new_down = (down[...] + ortho[2].T).astype(jnp.bfloat16)
    query = block_rows(second, 2, 2)
    gate_pre = dot(query, new_gate)
    up_pre = dot(query, new_up)
    hidden = (gate_pre * (1.0 / (1.0 + jnp.exp(-gate_pre))) * up_pre).astype(jnp.bfloat16)
    result = dot(hidden, new_down)
    span = result.shape[0]
    for column in range(FD // LANES):
        out[pl.ds(column, span, stride=FD // LANES), :] = result[
            :, column * LANES : (column + 1) * LANES
        ]


def call(kernel, shape, operands, flops, scalars=0, scratch=()):
    vmem = pl.BlockSpec(memory_space=pltpu.VMEM)
    smem = pl.BlockSpec(memory_space=pltpu.SMEM)
    return pl.pallas_call(
        kernel,
        out_shape=jax.ShapeDtypeStruct(shape, jnp.float32),
        in_specs=[smem] * scalars + [vmem] * (len(operands) - scalars),
        out_specs=vmem,
        scratch_shapes=scratch,
        compiler_params=pltpu.CompilerParams(vmem_limit_bytes=VMEM_LIMIT),
        cost_estimate=pl.CostEstimate(flops=flops, bytes_accessed=4 << 20, transcendentals=0),
    )(*operands)


def wide_index(x, half, y):
    return (x * HALVES + half) * YS + y


PLANES = [[wide_index(x, half, y) for x in range(XS) for y in range(YS)] for half in range(HALVES)]
SWAP = [
    (wide_index(x, half, y), wide_index(x, 1 - half, y))
    for x in range(XS)
    for half in range(HALVES)
    for y in range(YS)
]
AROUND = [
    (wide_index(x, half, y), wide_index(x, half, (y + 1) % YS))
    for x in range(XS)
    for half in range(HALVES)
    for y in range(YS)
]
ENDS = [(x, half, x + half, 1 - half) for x in range(XS) for half in range(HALVES)][:-1]
EDGE_LOW = [(wide_index(x, half, 0), wide_index(*after, 0)) for x, half, *after in ENDS]
EDGE_HIGH = [(wide_index(x, half, YS - 1), wide_index(*after, 0)) for x, half, *after in ENDS]
FLOPS = 1 << 20


def per_device(query_key, value_heads, fast_inputs, rate_logits, gate_fast, up_fast, down_fast):
    group = lax.axis_size("narrow")
    rows = query_key.shape[0]
    own = query_key.shape[1] // group
    span = rows * group
    pair = query_key.transpose(1, 0, 2).reshape(group, own * rows, 2 * LANES)
    value = value_heads.transpose(1, 0, 2).reshape(group, own * rows, LANES)
    fast = fast_inputs.transpose(1, 0, 2)
    fast = [fast[:, :, i * LANES : (i + 1) * LANES] for i in range(6)]
    logits = jnp.pad(rate_logits.transpose(1, 2, 0), ((0, 0), (0, 13), (0, LANES - rows)))
    first = jnp.concatenate([pair[:, :, LANES:], value, *fast[2:], logits], axis=1)
    second = jnp.concatenate([pair[:, :, :LANES], *fast[:2]], axis=1)
    first = lax.all_to_all(first, "narrow", 0, 0, tiled=True)
    tail = first[:, : 4 * rows]
    weights = (gate_fast[0], up_fast[0], down_fast[0])
    count = 3 * FHID // LANES * FD // PLANE
    pieces = call(gradient_kernel, (PLANE, count + 16, LANES), (first, *weights), FLOPS)
    got = lax.all_to_all(
        pieces.astype(jnp.float16), "wide", 0, 0, tiled=True, axis_index_groups=PLANES
    )
    got, tail, second = lax.optimization_barrier((got, tail, second))
    second = lax.all_to_all(second, "narrow", 0, 0, tiled=True)
    side = lax.ppermute(tail, "wide", AROUND)
    powers = got[:, count : count + 3].astype(jnp.float32)
    top = jnp.max(powers, axis=0)
    parts = got[:, :count].astype(jnp.float32).reshape(PLANE, 3, -1, LANES)
    half = jnp.sum(parts * (jnp.exp2(powers - top) * 0.0625)[:, :, None], axis=0)
    sent = jnp.concatenate(
        [half.reshape(count, LANES), top, jnp.zeros((13, LANES), jnp.float32)], axis=0
    )
    sent = sent.astype(jnp.float16)
    other = lax.ppermute(sent, "wide", SWAP)
    other, low_part, high_part = lax.optimization_barrier(
        (other, side[:, : 2 * rows], tail[:, 2 * rows :])
    )
    edge_low = lax.ppermute(low_part, "wide", EDGE_LOW)
    edge_high = lax.ppermute(high_part, "wide", EDGE_HIGH)
    other_top = other[count : count + 3].astype(jnp.float32)
    both = jnp.maximum(top, other_top)
    whole = half * (jnp.exp2(top - both) * 0.5)[:, None]
    whole = whole + other[:count].astype(jnp.float32).reshape(3, -1, LANES) * (
        jnp.exp2(other_top - both) * 0.5
    )[:, None]
    whole = whole.astype(jnp.float16).reshape(count, LANES)
    every = lax.all_gather(whole, "wide", axis_index_groups=PLANES)
    factors = jnp.concatenate([jnp.exp2(both - 8.0), jnp.zeros((5, LANES), jnp.float32)], axis=0)
    fast_out = call(
        apply_kernel,
        (span * FD // LANES, LANES),
        (factors, every.astype(jnp.float32), *weights, second),
        FLOPS,
    )
    place = lax.axis_index("wide").reshape(1)
    edge_low, edge_high, fast_out = lax.optimization_barrier((edge_low, edge_high, fast_out))
    window_out = call(
        attention_kernel,
        (span * own, LANES),
        (place, first, second, side, edge_low, edge_high),
        FLOPS,
        1,
        [pltpu.VMEM((PLANE, 4 * TOK, LANES), jnp.bfloat16)],
    )
    return (window_out.reshape(span, own, LANES), fast_out.reshape(span, 1, FD))


def solution(mesh):
    return jax.shard_map(
        per_device,
        mesh=mesh,
        in_specs=(
            P(("wide", "narrow"), None, None),
            P(("wide", "narrow"), None, None),
            P(("wide", "narrow"), None, None),
            P(("wide", "narrow"), None, None),
            P("narrow", None, None),
            P("narrow", None, None),
            P("narrow", None, None),
        ),
        out_specs=(P("wide", "narrow", None), P("wide", "narrow", None)),
        check_vma=False,
    )
```

```python
import math

import jax
import jax.numpy as jnp
from jax import lax
from jax.experimental import pallas as pl
from jax.experimental.pallas import tpu as pltpu
from jax.sharding import PartitionSpec as P

FD = 256
FHID = 512
WINDOW = 512
NS_STEPS = 5
LANES = 128
TOK = 32

coef_a = 3.4445
coef_b = -4.775
coef_c = 2.0315

XS, HALVES, YS = 4, 2, 4
PLANE = XS * YS
GROUP = 16
VMEM_LIMIT = 48 * 1024 * 1024


def dot(a, b, dims=((1,), (0,))):
    return lax.dot_general(a, b, (dims, ((), ())), preferred_element_type=jnp.float32)


def block_rows(ref, index, count):
    group = ref.shape[0]
    parts = [
        ref[:, (index + i) * TOK : (index + i + 1) * TOK, :].reshape(group * TOK, LANES)
        for i in range(count)
    ]
    return parts[0] if count == 1 else jnp.concatenate(parts, axis=1)


def gradient_kernel(first, gate, up, down, out):
    group = first.shape[0]
    span = group * TOK
    logits = first[:, 12 * TOK : 12 * TOK + 16, :].astype(jnp.float32)
    rate_blocks = []
    for source in range(group):
        turned = logits[source].T[:TOK]
        rate_blocks.append(jnp.maximum(turned, 0.0) + jnp.log1p(jnp.exp(-jnp.abs(turned))))
    rates = jnp.concatenate(rate_blocks, axis=0)
    key = block_rows(first, 4, 2)
    value = block_rows(first, 6, 2)
    gate_bf = gate[...].astype(jnp.bfloat16)
    up_bf = up[...].astype(jnp.bfloat16)
    down_bf = down[...].astype(jnp.bfloat16)
    totals = [None, None, None]
    half = span // 2
    for part in range(2):
        rows = slice(part * half, (part + 1) * half)
        key_part, value_part, rate = key[rows], value[rows], rates[rows]
        gate_pre = dot(key_part, gate_bf)
        up_pre = dot(key_part, up_bf)
        back = dot(value_part, down_bf, ((1,), (1,)))
        sigmoid_gate = 1.0 / (1.0 + jnp.exp(-gate_pre))
        activated = gate_pre * sigmoid_gate
        hidden = (activated * up_pre).astype(jnp.bfloat16)
        scaled_v = (rate[:, 1:2] * value_part.astype(jnp.float32)).astype(jnp.bfloat16)
        grad_gate = (
            rate[:, 0:1] * back * up_pre * sigmoid_gate * (1.0 + gate_pre * (1.0 - sigmoid_gate))
        ).astype(jnp.bfloat16)
        grad_up = (rate[:, 2:3] * back * activated).astype(jnp.bfloat16)
        fresh = (
            dot(key_part, grad_gate, ((0,), (0,))),
            dot(key_part, grad_up, ((0,), (0,))),
            dot(scaled_v, hidden, ((0,), (0,))),
        )
        totals = [new if old is None else old + new for old, new in zip(totals, fresh)]
    rows = FD // PLANE
    row = lax.broadcasted_iota(jnp.int32, (16, LANES), 0)
    tag = jnp.zeros((16, LANES), jnp.float32)
    for matrix, total in enumerate(totals):
        most = jnp.max(jnp.max(jnp.abs(total), axis=0, keepdims=True), axis=1, keepdims=True)
        power = jnp.floor(jnp.log(jnp.maximum(most, 1e-30)) * 1.4426950408889634)
        scaled = total * jnp.exp((13.0 - power) * 0.6931471805599453)
        tag = jnp.where(row == matrix, power, tag)
        for column in range(FHID // LANES):
            start = (matrix * (FHID // LANES) + column) * rows
            out[:, start : start + rows, :] = scaled[
                :, column * LANES : (column + 1) * LANES
            ].reshape(PLANE, rows, LANES)
    out[:, 3 * FHID // LANES * rows :, :] = jnp.broadcast_to(tag[None], (PLANE, 16, LANES))


def attention_kernel(place, first, side, edge, out, earlier):
    span = first.shape[0] * TOK
    scale = 1.0 / math.sqrt(LANES)
    tile = 128
    reach = span + tile
    row = lax.broadcasted_iota(jnp.int32, (tile, reach), 0)
    col = lax.broadcasted_iota(jnp.int32, (tile, reach), 1)
    band = (col > row) & (col - row <= span)
    begin = jnp.where(place[0] == 0, span, 0)
    on_edge = lax.rem(place[0], YS) == 0
    heads = 2

    @pl.when(on_edge)
    def _():
        earlier[...] = edge[...]

    @pl.when(jnp.logical_not(on_edge))
    def _():
        earlier[...] = side[...]

    for head in range(heads):
        query = block_rows(first, 8 + head, 1)
        key = jnp.concatenate([block_rows(earlier, head, 1), block_rows(first, head, 1)], axis=0)
        value = jnp.concatenate(
            [block_rows(earlier, heads + head, 1), block_rows(first, heads + head, 1)], axis=0
        )
        for step in range(span // tile):
            low = step * tile
            scores = dot(query[low : low + tile], key[low : low + reach], ((1,), (1,))) * scale
            keep = band & (col + low >= begin)
            scores = jnp.where(keep, scores, -1e30)
            terms = jnp.exp(scores - jnp.max(scores, axis=1, keepdims=True))
            probs = (terms * (1.0 / jnp.sum(terms, axis=1, keepdims=True))).astype(jnp.bfloat16)
            out[pl.ds(low * heads + head, tile, stride=heads), :] = dot(
                probs, value[low : low + reach]
            )


def split(a):
    high = a.astype(jnp.bfloat16)
    return high, (a - high.astype(jnp.float32)).astype(jnp.bfloat16)


def orthogonal(ortho_all):
    for _ in range(NS_STEPS):
        grams, polys, nexts = [], [], []
        halves = [split(ortho) for ortho in ortho_all]
        for high, low in halves:
            cross = dot(high, low, ((1,), (1,)))
            grams.append(dot(high, high, ((1,), (1,))) + (cross + cross.T))
        for gram in grams:
            high, low = split(gram)
            square = dot(high, high) + (dot(high, low) + dot(low, high))
            polys.append(coef_b * gram + coef_c * square)
        for ortho, poly, (high, low) in zip(ortho_all, polys, halves):
            top, rest = split(poly)
            nexts.append(coef_a * ortho + (dot(top, high) + (dot(top, low) + dot(rest, high))))
        ortho_all = nexts
    return ortho_all


def apply_kernel(powers, every, gate, up, down, first, out):
    rows = FD // PLANE
    starts = []
    for matrix in range(3):
        columns = []
        for column in range(FHID // LANES):
            start = (matrix * (FHID // LANES) + column) * rows
            columns.append(every[:, start : start + rows, :].reshape(FD, LANES))
        total = jnp.concatenate(columns, axis=1)
        squares = jnp.sum(jnp.sum(total * total, axis=0, keepdims=True), axis=1, keepdims=True)
        factor = powers[matrix : matrix + 1, 0:1]
        starts.append(total * (factor / jnp.sqrt(squares * factor * factor + 1e-6)))
    ortho = orthogonal(starts)
    new_gate = (gate[...] + ortho[0]).astype(jnp.bfloat16)
    new_up = (up[...] + ortho[1]).astype(jnp.bfloat16)
    new_down = (down[...] + ortho[2].T).astype(jnp.bfloat16)
    query = block_rows(first, 10, 2)
    gate_pre = dot(query, new_gate)
    up_pre = dot(query, new_up)
    hidden = (gate_pre * (1.0 / (1.0 + jnp.exp(-gate_pre))) * up_pre).astype(jnp.bfloat16)
    result = dot(hidden, new_down)
    span = result.shape[0]
    for column in range(FD // LANES):
        out[pl.ds(column, span, stride=FD // LANES), :] = result[
            :, column * LANES : (column + 1) * LANES
        ]


def call(kernel, shape, operands, flops, scalars=0, scratch=()):
    vmem = pl.BlockSpec(memory_space=pltpu.VMEM)
    smem = pl.BlockSpec(memory_space=pltpu.SMEM)
    return pl.pallas_call(
        kernel,
        out_shape=jax.ShapeDtypeStruct(shape, jnp.float32),
        in_specs=[smem] * scalars + [vmem] * (len(operands) - scalars),
        out_specs=vmem,
        scratch_shapes=scratch,
        compiler_params=pltpu.CompilerParams(vmem_limit_bytes=VMEM_LIMIT),
        cost_estimate=pl.CostEstimate(flops=flops, bytes_accessed=4 << 20, transcendentals=0),
    )(*operands)


def wide_index(x, half, y):
    return (x * HALVES + half) * YS + y


PLANES = [[wide_index(x, half, y) for x in range(XS) for y in range(YS)] for half in range(HALVES)]
SWAP = [
    (wide_index(x, half, y), wide_index(x, 1 - half, y))
    for x in range(XS)
    for half in range(HALVES)
    for y in range(YS)
]
LINES = [(x, half) for x in range(XS) for half in range(HALVES)]
NEXT = [
    (wide_index(*line, y), wide_index(*line, y + 1)) for line in LINES for y in range(YS - 1)
]
RELAY = [
    [(wide_index(*line, YS - 1), wide_index(*line, y)) for line in LINES] for y in range(YS - 1)
]
ENDS = [(x, half, x + half, 1 - half) for x in range(XS) for half in range(HALVES)][:-1]


def other_core(pairs):
    return [
        (a * GROUP + i, b * GROUP + (i ^ 1)) for a, b in pairs for i in range(GROUP)
    ]


EDGES = [
    other_core([(wide_index(x, half, y), wide_index(*after, 0)) for x, half, *after in ENDS])
    for y in range(YS)
]
CORES = other_core([(wide_index(*line, 0), wide_index(*line, 0)) for line in LINES])
FLOPS = 1 << 20


def per_device(query_key, value_heads, fast_inputs, rate_logits, gate_fast, up_fast, down_fast):
    group = lax.axis_size("narrow")
    rows = query_key.shape[0]
    own = query_key.shape[1] // group
    span = rows * group
    pair = query_key.transpose(1, 0, 2).reshape(group, own * rows, 2 * LANES)
    value = value_heads.transpose(1, 0, 2).reshape(group, own * rows, LANES)
    fast = fast_inputs.transpose(1, 0, 2)
    fast = [fast[:, :, i * LANES : (i + 1) * LANES] for i in range(6)]
    logits = jnp.pad(rate_logits.transpose(1, 2, 0), ((0, 0), (0, 13), (0, LANES - rows)))
    first = jnp.concatenate(
        [pair[:, :, LANES:], value, *fast[2:], pair[:, :, :LANES], *fast[:2], logits], axis=1
    )
    first = lax.all_to_all(first, "narrow", 0, 0, tiled=True)
    tail = first[:, : 4 * rows]
    quarters = [first[:, i * rows : (i + 1) * rows] for i in range(YS)]
    quarters = [
        lax.ppermute(part, "wide", pairs) for part, pairs in zip(quarters, RELAY)
    ] + quarters[-1:]

    weights = (gate_fast[0], up_fast[0], down_fast[0])
    count = 3 * FHID // LANES * FD // PLANE
    pieces = call(gradient_kernel, (PLANE, count + 16, LANES), (first, *weights), FLOPS)
    got = lax.all_to_all(
        pieces.astype(jnp.float16), "wide", 0, 0, tiled=True, axis_index_groups=PLANES
    )
    got, tail, quarters = lax.optimization_barrier((got, tail, quarters))
    edges = [
        lax.ppermute(part, ("wide", "narrow"), pairs) for part, pairs in zip(quarters, EDGES)
    ]
    side = lax.ppermute(tail, "wide", NEXT)
    powers = got[:, count : count + 3].astype(jnp.float32)
    top = jnp.max(powers, axis=0)
    parts = got[:, :count].astype(jnp.float32).reshape(PLANE, 3, -1, LANES)
    half = jnp.sum(parts * (jnp.exp2(powers - top) * 0.0625)[:, :, None], axis=0)
    sent = jnp.concatenate(
        [half.reshape(count, LANES), top, jnp.zeros((13, LANES), jnp.float32)], axis=0
    )
    sent = sent.astype(jnp.float16)
    other = lax.ppermute(sent, "wide", SWAP)
    other, side = lax.optimization_barrier((other, side))
    other_top = other[count : count + 3].astype(jnp.float32)
    both = jnp.maximum(top, other_top)
    whole = half * (jnp.exp2(top - both) * 0.5)[:, None]
    whole = whole + other[:count].astype(jnp.float32).reshape(3, -1, LANES) * (
        jnp.exp2(other_top - both) * 0.5
    )[:, None]
    whole = whole.astype(jnp.float16).reshape(count, LANES)
    every = lax.all_to_all(
        jnp.broadcast_to(whole[None], (PLANE, count, LANES)),
        "wide",
        0,
        0,
        tiled=True,
        axis_index_groups=PLANES,
    )
    edge = jnp.concatenate(edges, axis=1)
    edge = lax.ppermute(edge, ("wide", "narrow"), CORES)
    factors = jnp.concatenate([jnp.exp2(both - 8.0), jnp.zeros((5, LANES), jnp.float32)], axis=0)
    fast_out = call(
        apply_kernel,
        (span * FD // LANES, LANES),
        (factors, every.astype(jnp.float32), *weights, first),
        FLOPS,
    )
    place = lax.axis_index("wide").reshape(1)
    edge, fast_out = lax.optimization_barrier((edge, fast_out))
    window_out = call(
        attention_kernel,
        (span * own, LANES),
        (place, first, side, edge),
        FLOPS,
        1,
        [pltpu.VMEM((PLANE, 4 * TOK, LANES), jnp.bfloat16)],
    )
    return (window_out.reshape(span, own, LANES), fast_out.reshape(span, 1, FD))


def solution(mesh):
    return jax.shard_map(
        per_device,
        mesh=mesh,
        in_specs=(
            P(("wide", "narrow"), None, None),
            P(("wide", "narrow"), None, None),
            P(("wide", "narrow"), None, None),
            P(("wide", "narrow"), None, None),
            P("narrow", None, None),
            P("narrow", None, None),
            P("narrow", None, None),
        ),
        out_specs=(P("wide", "narrow", None), P("wide", "narrow", None)),
        check_vma=False,
    )
```

```python
import math

import jax
import jax.numpy as jnp
from jax import lax
from jax.experimental import pallas as pl
from jax.experimental.pallas import tpu as pltpu
from jax.sharding import PartitionSpec as P

FD = 256
FHID = 512
WINDOW = 512
NS_STEPS = 5
LANES = 128
TOK = 32

coef_a = 3.4445
coef_b = -4.775
coef_c = 2.0315

XS, HALVES, YS = 4, 2, 4
PLANE = XS * YS
VMEM_LIMIT = 48 * 1024 * 1024


def dot(a, b, dims=((1,), (0,))):
    return lax.dot_general(a, b, (dims, ((), ())), preferred_element_type=jnp.float32)


def block_rows(ref, index, count):
    group = ref.shape[0]
    parts = [
        ref[:, (index + i) * TOK : (index + i + 1) * TOK, :].reshape(group * TOK, LANES)
        for i in range(count)
    ]
    return parts[0] if count == 1 else jnp.concatenate(parts, axis=1)


def gradient_kernel(first, gate, up, down, out):
    group = first.shape[0]
    span = group * TOK
    logits = first[:, 12 * TOK : 12 * TOK + 16, :].astype(jnp.float32)
    rate_blocks = []
    for source in range(group):
        turned = logits[source].T[:TOK]
        rate_blocks.append(jnp.maximum(turned, 0.0) + jnp.log1p(jnp.exp(-jnp.abs(turned))))
    rates = jnp.concatenate(rate_blocks, axis=0)
    key = block_rows(first, 4, 2)
    value = block_rows(first, 6, 2)
    gate_bf = gate[...].astype(jnp.bfloat16)
    up_bf = up[...].astype(jnp.bfloat16)
    down_bf = down[...].astype(jnp.bfloat16)
    totals = [None, None, None]
    half = span // 2
    for part in range(2):
        rows = slice(part * half, (part + 1) * half)
        key_part, value_part, rate = key[rows], value[rows], rates[rows]
        gate_pre = dot(key_part, gate_bf)
        up_pre = dot(key_part, up_bf)
        back = dot(value_part, down_bf, ((1,), (1,)))
        sigmoid_gate = 1.0 / (1.0 + jnp.exp(-gate_pre))
        activated = gate_pre * sigmoid_gate
        hidden = (activated * up_pre).astype(jnp.bfloat16)
        scaled_v = (rate[:, 1:2] * value_part.astype(jnp.float32)).astype(jnp.bfloat16)
        grad_gate = (
            rate[:, 0:1] * back * up_pre * sigmoid_gate * (1.0 + gate_pre * (1.0 - sigmoid_gate))
        ).astype(jnp.bfloat16)
        grad_up = (rate[:, 2:3] * back * activated).astype(jnp.bfloat16)
        fresh = (
            dot(key_part, grad_gate, ((0,), (0,))),
            dot(key_part, grad_up, ((0,), (0,))),
            dot(scaled_v, hidden, ((0,), (0,))),
        )
        totals = [new if old is None else old + new for old, new in zip(totals, fresh)]
    rows = FD // PLANE
    row = lax.broadcasted_iota(jnp.int32, (16, LANES), 0)
    tag = jnp.zeros((16, LANES), jnp.float32)
    for matrix, total in enumerate(totals):
        most = jnp.max(jnp.max(jnp.abs(total), axis=0, keepdims=True), axis=1, keepdims=True)
        power = jnp.floor(jnp.log(jnp.maximum(most, 1e-30)) * 1.4426950408889634)
        scaled = total * jnp.exp((13.0 - power) * 0.6931471805599453)
        tag = jnp.where(row == matrix, power, tag)
        for column in range(FHID // LANES):
            start = (matrix * (FHID // LANES) + column) * rows
            out[:, start : start + rows, :] = scaled[
                :, column * LANES : (column + 1) * LANES
            ].reshape(PLANE, rows, LANES)
    out[:, 3 * FHID // LANES * rows :, :] = jnp.broadcast_to(tag[None], (PLANE, 16, LANES))


def attention_kernel(place, first, side, edge0, edge1, edge2, edge3, out, earlier):
    span = first.shape[0] * TOK
    scale = 1.0 / math.sqrt(LANES)
    tile = 128
    reach = span + tile
    row = lax.broadcasted_iota(jnp.int32, (tile, reach), 0)
    col = lax.broadcasted_iota(jnp.int32, (tile, reach), 1)
    band = (col > row) & (col - row <= span)
    begin = jnp.where(place[0] == 0, span, 0)
    on_edge = lax.rem(place[0], YS) == 0
    heads = 2

    @pl.when(on_edge)
    def _():
        for i, edge in enumerate((edge0, edge1, edge2, edge3)):
            earlier[:, i * TOK : (i + 1) * TOK, :] = edge[...]

    @pl.when(jnp.logical_not(on_edge))
    def _():
        earlier[...] = side[...]

    for head in range(heads):
        query = block_rows(first, 8 + head, 1)
        key = jnp.concatenate([block_rows(earlier, head, 1), block_rows(first, head, 1)], axis=0)
        value = jnp.concatenate(
            [block_rows(earlier, heads + head, 1), block_rows(first, heads + head, 1)], axis=0
        )
        for step in range(span // tile):
            low = step * tile
            scores = dot(query[low : low + tile], key[low : low + reach], ((1,), (1,))) * scale
            keep = band & (col + low >= begin)
            scores = jnp.where(keep, scores, -1e30)
            terms = jnp.exp(scores - jnp.max(scores, axis=1, keepdims=True))
            probs = (terms * (1.0 / jnp.sum(terms, axis=1, keepdims=True))).astype(jnp.bfloat16)
            out[pl.ds(low * heads + head, tile, stride=heads), :] = dot(
                probs, value[low : low + reach]
            )


def split(a):
    high = a.astype(jnp.bfloat16)
    return high, (a - high.astype(jnp.float32)).astype(jnp.bfloat16)


def orthogonal(ortho_all):
    for _ in range(NS_STEPS):
        grams, polys, nexts = [], [], []
        halves = [split(ortho) for ortho in ortho_all]
        for high, low in halves:
            cross = dot(high, low, ((1,), (1,)))
            grams.append(dot(high, high, ((1,), (1,))) + (cross + cross.T))
        for gram in grams:
            high, low = split(gram)
            square = dot(high, high) + (dot(high, low) + dot(low, high))
            polys.append(coef_b * gram + coef_c * square)
        for ortho, poly, (high, low) in zip(ortho_all, polys, halves):
            top, rest = split(poly)
            nexts.append(coef_a * ortho + (dot(top, high) + (dot(top, low) + dot(rest, high))))
        ortho_all = nexts
    return ortho_all


def apply_kernel(powers, every, gate, up, down, first, out):
    rows = FD // PLANE
    starts = []
    for matrix in range(3):
        columns = []
        for column in range(FHID // LANES):
            start = (matrix * (FHID // LANES) + column) * rows
            columns.append(every[:, start : start + rows, :].reshape(FD, LANES))
        total = jnp.concatenate(columns, axis=1)
        squares = jnp.sum(jnp.sum(total * total, axis=0, keepdims=True), axis=1, keepdims=True)
        factor = powers[matrix : matrix + 1, 0:1]
        starts.append(total * (factor / jnp.sqrt(squares * factor * factor + 1e-6)))
    ortho = orthogonal(starts)
    new_gate = (gate[...] + ortho[0]).astype(jnp.bfloat16)
    new_up = (up[...] + ortho[1]).astype(jnp.bfloat16)
    new_down = (down[...] + ortho[2].T).astype(jnp.bfloat16)
    query = block_rows(first, 10, 2)
    gate_pre = dot(query, new_gate)
    up_pre = dot(query, new_up)
    hidden = (gate_pre * (1.0 / (1.0 + jnp.exp(-gate_pre))) * up_pre).astype(jnp.bfloat16)
    result = dot(hidden, new_down)
    span = result.shape[0]
    for column in range(FD // LANES):
        out[pl.ds(column, span, stride=FD // LANES), :] = result[
            :, column * LANES : (column + 1) * LANES
        ]


def call(kernel, shape, operands, flops, scalars=0, scratch=()):
    vmem = pl.BlockSpec(memory_space=pltpu.VMEM)
    smem = pl.BlockSpec(memory_space=pltpu.SMEM)
    return pl.pallas_call(
        kernel,
        out_shape=jax.ShapeDtypeStruct(shape, jnp.float32),
        in_specs=[smem] * scalars + [vmem] * (len(operands) - scalars),
        out_specs=vmem,
        scratch_shapes=scratch,
        compiler_params=pltpu.CompilerParams(vmem_limit_bytes=VMEM_LIMIT),
        cost_estimate=pl.CostEstimate(flops=flops, bytes_accessed=4 << 20, transcendentals=0),
    )(*operands)


def wide_index(x, half, y):
    return (x * HALVES + half) * YS + y


PLANES = [[wide_index(x, half, y) for x in range(XS) for y in range(YS)] for half in range(HALVES)]
SWAP = [
    (wide_index(x, half, y), wide_index(x, 1 - half, y))
    for x in range(XS)
    for half in range(HALVES)
    for y in range(YS)
]
LINES = [(x, half) for x in range(XS) for half in range(HALVES)]
NEXT = [
    (wide_index(*line, y), wide_index(*line, y + 1)) for line in LINES for y in range(YS - 1)
]
RELAY = [
    [(wide_index(*line, YS - 1), wide_index(*line, y)) for line in LINES] for y in range(YS - 1)
]
ENDS = [(x, half, x + half, 1 - half) for x in range(XS) for half in range(HALVES)][:-1]

EDGES = [
    [(wide_index(x, half, y), wide_index(*after, 0)) for x, half, *after in ENDS]
    for y in range(YS)
]
FLOPS = 1 << 20


def per_device(query_key, value_heads, fast_inputs, rate_logits, gate_fast, up_fast, down_fast):
    group = lax.axis_size("narrow")
    rows = query_key.shape[0]
    own = query_key.shape[1] // group
    span = rows * group
    pair = query_key.transpose(1, 0, 2).reshape(group, own * rows, 2 * LANES)
    value = value_heads.transpose(1, 0, 2).reshape(group, own * rows, LANES)
    fast = fast_inputs.transpose(1, 0, 2)
    fast = [fast[:, :, i * LANES : (i + 1) * LANES] for i in range(6)]
    logits = jnp.pad(rate_logits.transpose(1, 2, 0), ((0, 0), (0, 13), (0, LANES - rows)))
    first = jnp.concatenate(
        [pair[:, :, LANES:], value, *fast[2:], pair[:, :, :LANES], *fast[:2], logits], axis=1
    )
    first = lax.all_to_all(first, "narrow", 0, 0, tiled=True)
    tail = first[:, : 4 * rows]
    quarters = [first[:, i * rows : (i + 1) * rows] for i in range(YS)]
    quarters = [
        lax.ppermute(part, "wide", pairs) for part, pairs in zip(quarters, RELAY)
    ] + quarters[-1:]

    weights = (gate_fast[0], up_fast[0], down_fast[0])
    count = 3 * FHID // LANES * FD // PLANE
    pieces = call(gradient_kernel, (PLANE, count + 16, LANES), (first, *weights), FLOPS)
    got = lax.all_to_all(
        pieces.astype(jnp.float16), "wide", 0, 0, tiled=True, axis_index_groups=PLANES
    )
    got, tail, quarters = lax.optimization_barrier((got, tail, quarters))
    side = lax.ppermute(tail, "wide", NEXT)
    powers = got[:, count : count + 3].astype(jnp.float32)
    top = jnp.max(powers, axis=0)
    parts = got[:, :count].astype(jnp.float32).reshape(PLANE, 3, -1, LANES)
    half = jnp.sum(parts * (jnp.exp2(powers - top) * 0.0625)[:, :, None], axis=0)
    sent = jnp.concatenate(
        [half.reshape(count, LANES), top, jnp.zeros((13, LANES), jnp.float32)], axis=0
    )
    sent = sent.astype(jnp.float16)
    other = lax.ppermute(sent, "wide", SWAP)
    other, side, quarters = lax.optimization_barrier((other, side, quarters))
    edges = [lax.ppermute(part, "wide", pairs) for part, pairs in zip(quarters, EDGES)]
    other_top = other[count : count + 3].astype(jnp.float32)
    both = jnp.maximum(top, other_top)
    whole = half * (jnp.exp2(top - both) * 0.5)[:, None]
    whole = whole + other[:count].astype(jnp.float32).reshape(3, -1, LANES) * (
        jnp.exp2(other_top - both) * 0.5
    )[:, None]
    whole = whole.astype(jnp.float16).reshape(count, LANES)
    every = lax.all_to_all(
        jnp.broadcast_to(whole[None], (PLANE, count, LANES)),
        "wide",
        0,
        0,
        tiled=True,
        axis_index_groups=PLANES,
    )
    factors = jnp.concatenate([jnp.exp2(both - 8.0), jnp.zeros((5, LANES), jnp.float32)], axis=0)
    fast_out = call(
        apply_kernel,
        (span * FD // LANES, LANES),
        (factors, every.astype(jnp.float32), *weights, first),
        FLOPS,
    )
    place = lax.axis_index("wide").reshape(1)
    edges, fast_out = lax.optimization_barrier((edges, fast_out))
    window_out = call(
        attention_kernel,
        (span * own, LANES),
        (place, first, side, *edges),
        FLOPS,
        1,
        [pltpu.VMEM((PLANE, 4 * TOK, LANES), jnp.bfloat16)],
    )
    return (window_out.reshape(span, own, LANES), fast_out.reshape(span, 1, FD))


def solution(mesh):
    return jax.shard_map(
        per_device,
        mesh=mesh,
        in_specs=(
            P(("wide", "narrow"), None, None),
            P(("wide", "narrow"), None, None),
            P(("wide", "narrow"), None, None),
            P(("wide", "narrow"), None, None),
            P("narrow", None, None),
            P("narrow", None, None),
            P("narrow", None, None),
        ),
        out_specs=(P("wide", "narrow", None), P("wide", "narrow", None)),
        check_vma=False,
    )
```

```python
import math

import jax
import jax.numpy as jnp
from jax import lax
from jax.experimental import pallas as pl
from jax.experimental.pallas import tpu as pltpu
from jax.sharding import PartitionSpec as P

FD = 256
FHID = 512
WINDOW = 512
NS_STEPS = 5
LANES = 128
TOK = 32

coef_a = 3.4445
coef_b = -4.775
coef_c = 2.0315

XS, HALVES, YS = 4, 2, 4
PLANE = XS * YS
CUT = 80
VMEM_LIMIT = 48 * 1024 * 1024


def dot(a, b, dims=((1,), (0,))):
    return lax.dot_general(a, b, (dims, ((), ())), preferred_element_type=jnp.float32)


def block_rows(ref, index, count):
    group = ref.shape[0]
    parts = [
        ref[:, (index + i) * TOK : (index + i + 1) * TOK, :].reshape(group * TOK, LANES)
        for i in range(count)
    ]
    return parts[0] if count == 1 else jnp.concatenate(parts, axis=1)


def gradient_kernel(first, gate, up, down, out):
    group = first.shape[0]
    span = group * TOK
    logits = first[:, 12 * TOK : 12 * TOK + 16, :].astype(jnp.float32)
    rate_blocks = []
    for source in range(group):
        turned = logits[source].T[:TOK]
        rate_blocks.append(jnp.maximum(turned, 0.0) + jnp.log1p(jnp.exp(-jnp.abs(turned))))
    rates = jnp.concatenate(rate_blocks, axis=0)
    key = block_rows(first, 4, 2)
    value = block_rows(first, 6, 2)
    gate_bf = gate[...].astype(jnp.bfloat16)
    up_bf = up[...].astype(jnp.bfloat16)
    down_bf = down[...].astype(jnp.bfloat16)
    totals = [None, None, None]
    half = span // 2
    for part in range(2):
        rows = slice(part * half, (part + 1) * half)
        key_part, value_part, rate = key[rows], value[rows], rates[rows]
        gate_pre = dot(key_part, gate_bf)
        up_pre = dot(key_part, up_bf)
        back = dot(value_part, down_bf, ((1,), (1,)))
        sigmoid_gate = 1.0 / (1.0 + jnp.exp(-gate_pre))
        activated = gate_pre * sigmoid_gate
        hidden = (activated * up_pre).astype(jnp.bfloat16)
        scaled_v = (rate[:, 1:2] * value_part.astype(jnp.float32)).astype(jnp.bfloat16)
        grad_gate = (
            rate[:, 0:1] * back * up_pre * sigmoid_gate * (1.0 + gate_pre * (1.0 - sigmoid_gate))
        ).astype(jnp.bfloat16)
        grad_up = (rate[:, 2:3] * back * activated).astype(jnp.bfloat16)
        fresh = (
            dot(key_part, grad_gate, ((0,), (0,))),
            dot(key_part, grad_up, ((0,), (0,))),
            dot(scaled_v, hidden, ((0,), (0,))),
        )
        totals = [new if old is None else old + new for old, new in zip(totals, fresh)]
    rows = FD // PLANE
    row = lax.broadcasted_iota(jnp.int32, (16, LANES), 0)
    tag = jnp.zeros((16, LANES), jnp.float32)
    for matrix, total in enumerate(totals):
        most = jnp.max(jnp.max(jnp.abs(total), axis=0, keepdims=True), axis=1, keepdims=True)
        power = jnp.floor(jnp.log(jnp.maximum(most, 1e-30)) * 1.4426950408889634)
        scaled = total * jnp.exp((13.0 - power) * 0.6931471805599453)
        tag = jnp.where(row == matrix, power, tag)
        for column in range(FHID // LANES):
            start = (matrix * (FHID // LANES) + column) * rows
            out[:, start : start + rows, :] = scaled[
                :, column * LANES : (column + 1) * LANES
            ].reshape(PLANE, rows, LANES)
    out[:, 3 * FHID // LANES * rows :, :] = jnp.broadcast_to(tag[None], (PLANE, 16, LANES))


def attention_kernel(place, first, side, edge_low, edge_high, out, earlier):
    span = first.shape[0] * TOK
    scale = 1.0 / math.sqrt(LANES)
    tile = 128
    reach = span + tile
    row = lax.broadcasted_iota(jnp.int32, (tile, reach), 0)
    col = lax.broadcasted_iota(jnp.int32, (tile, reach), 1)
    band = (col > row) & (col - row <= span)
    begin = jnp.where(place[0] == 0, span, 0)
    edge = lax.rem(place[0], YS) == 0
    heads = 2

    @pl.when(edge)
    def _():
        earlier[:, :CUT, :] = edge_low[...]
        earlier[:, CUT:, :] = edge_high[...]

    @pl.when(jnp.logical_not(edge))
    def _():
        earlier[...] = side[...]

    for head in range(heads):
        query = block_rows(first, 8 + head, 1)
        key = jnp.concatenate([block_rows(earlier, head, 1), block_rows(first, head, 1)], axis=0)
        value = jnp.concatenate(
            [block_rows(earlier, heads + head, 1), block_rows(first, heads + head, 1)], axis=0
        )
        for step in range(span // tile):
            low = step * tile
            scores = dot(query[low : low + tile], key[low : low + reach], ((1,), (1,))) * scale
            keep = band & (col + low >= begin)
            scores = jnp.where(keep, scores, -1e30)
            terms = jnp.exp(scores - jnp.max(scores, axis=1, keepdims=True))
            probs = (terms * (1.0 / jnp.sum(terms, axis=1, keepdims=True))).astype(jnp.bfloat16)
            out[pl.ds(low * heads + head, tile, stride=heads), :] = dot(
                probs, value[low : low + reach]
            )


def split(a):
    high = a.astype(jnp.bfloat16)
    return high, (a - high.astype(jnp.float32)).astype(jnp.bfloat16)


def orthogonal(ortho_all):
    for _ in range(NS_STEPS):
        grams, polys, nexts = [], [], []
        halves = [split(ortho) for ortho in ortho_all]
        for high, low in halves:
            cross = dot(high, low, ((1,), (1,)))
            grams.append(dot(high, high, ((1,), (1,))) + (cross + cross.T))
        for gram in grams:
            high, low = split(gram)
            square = dot(high, high) + (dot(high, low) + dot(low, high))
            polys.append(coef_b * gram + coef_c * square)
        for ortho, poly, (high, low) in zip(ortho_all, polys, halves):
            top, rest = split(poly)
            nexts.append(coef_a * ortho + (dot(top, high) + (dot(top, low) + dot(rest, high))))
        ortho_all = nexts
    return ortho_all


def apply_kernel(powers, every, gate, up, down, first, out):
    rows = FD // PLANE
    starts = []
    for matrix in range(3):
        columns = []
        for column in range(FHID // LANES):
            start = (matrix * (FHID // LANES) + column) * rows
            columns.append(every[:, start : start + rows, :].reshape(FD, LANES))
        total = jnp.concatenate(columns, axis=1)
        squares = jnp.sum(jnp.sum(total * total, axis=0, keepdims=True), axis=1, keepdims=True)
        factor = powers[matrix : matrix + 1, 0:1]
        starts.append(total * (factor / jnp.sqrt(squares * factor * factor + 1e-6)))
    ortho = orthogonal(starts)
    new_gate = (gate[...] + ortho[0]).astype(jnp.bfloat16)
    new_up = (up[...] + ortho[1]).astype(jnp.bfloat16)
    new_down = (down[...] + ortho[2].T).astype(jnp.bfloat16)
    query = block_rows(first, 10, 2)
    gate_pre = dot(query, new_gate)
    up_pre = dot(query, new_up)
    hidden = (gate_pre * (1.0 / (1.0 + jnp.exp(-gate_pre))) * up_pre).astype(jnp.bfloat16)
    result = dot(hidden, new_down)
    span = result.shape[0]
    for column in range(FD // LANES):
        out[pl.ds(column, span, stride=FD // LANES), :] = result[
            :, column * LANES : (column + 1) * LANES
        ]


def call(kernel, shape, operands, flops, scalars=0, scratch=()):
    vmem = pl.BlockSpec(memory_space=pltpu.VMEM)
    smem = pl.BlockSpec(memory_space=pltpu.SMEM)
    return pl.pallas_call(
        kernel,
        out_shape=jax.ShapeDtypeStruct(shape, jnp.float32),
        in_specs=[smem] * scalars + [vmem] * (len(operands) - scalars),
        out_specs=vmem,
        scratch_shapes=scratch,
        compiler_params=pltpu.CompilerParams(vmem_limit_bytes=VMEM_LIMIT),
        cost_estimate=pl.CostEstimate(flops=flops, bytes_accessed=4 << 20, transcendentals=0),
    )(*operands)


def wide_index(x, half, y):
    return (x * HALVES + half) * YS + y


PLANES = [[wide_index(x, half, y) for x in range(XS) for y in range(YS)] for half in range(HALVES)]
SWAP = [
    (wide_index(x, half, y), wide_index(x, 1 - half, y))
    for x in range(XS)
    for half in range(HALVES)
    for y in range(YS)
]
AROUND = [
    (wide_index(x, half, y), wide_index(x, half, (y + 1) % YS))
    for x in range(XS)
    for half in range(HALVES)
    for y in range(YS)
]
ENDS = [(x, half, x + half, 1 - half) for x in range(XS) for half in range(HALVES)][:-1]
EDGE_LOW = [(wide_index(x, half, 0), wide_index(*after, 0)) for x, half, *after in ENDS]
EDGE_HIGH = [(wide_index(x, half, YS - 1), wide_index(*after, 0)) for x, half, *after in ENDS]
FLOPS = 1 << 20


def per_device(query_key, value_heads, fast_inputs, rate_logits, gate_fast, up_fast, down_fast):
    group = lax.axis_size("narrow")
    rows = query_key.shape[0]
    own = query_key.shape[1] // group
    span = rows * group
    pair = query_key.transpose(1, 0, 2).reshape(group, own * rows, 2 * LANES)
    value = value_heads.transpose(1, 0, 2).reshape(group, own * rows, LANES)
    fast = fast_inputs.transpose(1, 0, 2)
    fast = [fast[:, :, i * LANES : (i + 1) * LANES] for i in range(6)]
    logits = jnp.pad(rate_logits.transpose(1, 2, 0), ((0, 0), (0, 13), (0, LANES - rows)))
    first = jnp.concatenate(
        [pair[:, :, LANES:], value, *fast[2:], pair[:, :, :LANES], *fast[:2], logits], axis=1
    )
    first = lax.all_to_all(first, "narrow", 0, 0, tiled=True)
    tail = first[:, : 4 * rows]
    edge_high = lax.ppermute(first[:, CUT : 4 * rows], "wide", EDGE_HIGH)

    weights = (gate_fast[0], up_fast[0], down_fast[0])
    count = 3 * FHID // LANES * FD // PLANE
    pieces = call(gradient_kernel, (PLANE, count + 16, LANES), (first, *weights), FLOPS)
    got = lax.all_to_all(
        pieces.astype(jnp.float16), "wide", 0, 0, tiled=True, axis_index_groups=PLANES
    )
    got, tail = lax.optimization_barrier((got, tail))
    side = lax.ppermute(tail, "wide", AROUND)
    powers = got[:, count : count + 3].astype(jnp.float32)
    top = jnp.max(powers, axis=0)
    parts = got[:, :count].astype(jnp.float32).reshape(PLANE, 3, -1, LANES)
    half = jnp.sum(parts * (jnp.exp2(powers - top) * 0.0625)[:, :, None], axis=0)
    sent = jnp.concatenate(
        [half.reshape(count, LANES), top, jnp.zeros((13, LANES), jnp.float32)], axis=0
    )
    sent = sent.astype(jnp.float16)
    other = lax.ppermute(sent, "wide", SWAP)
    other, low_part, edge_high = lax.optimization_barrier((other, side[:, :CUT], edge_high))
    edge_low = lax.ppermute(low_part, "wide", EDGE_LOW)
    other_top = other[count : count + 3].astype(jnp.float32)
    both = jnp.maximum(top, other_top)
    whole = half * (jnp.exp2(top - both) * 0.5)[:, None]
    whole = whole + other[:count].astype(jnp.float32).reshape(3, -1, LANES) * (
        jnp.exp2(other_top - both) * 0.5
    )[:, None]
    whole = whole.astype(jnp.float16).reshape(count, LANES)
    every = lax.all_to_all(
        jnp.broadcast_to(whole[None], (PLANE, count, LANES)),
        "wide",
        0,
        0,
        tiled=True,
        axis_index_groups=PLANES,
    )
    factors = jnp.concatenate([jnp.exp2(both - 8.0), jnp.zeros((5, LANES), jnp.float32)], axis=0)
    fast_out = call(
        apply_kernel,
        (span * FD // LANES, LANES),
        (factors, every.astype(jnp.float32), *weights, first),
        FLOPS,
    )
    place = lax.axis_index("wide").reshape(1)
    edge_low, fast_out = lax.optimization_barrier((edge_low, fast_out))
    window_out = call(
        attention_kernel,
        (span * own, LANES),
        (place, first, side, edge_low, edge_high),
        FLOPS,
        1,
        [pltpu.VMEM((PLANE, 4 * TOK, LANES), jnp.bfloat16)],
    )
    return (window_out.reshape(span, own, LANES), fast_out.reshape(span, 1, FD))


def solution(mesh):
    return jax.shard_map(
        per_device,
        mesh=mesh,
        in_specs=(
            P(("wide", "narrow"), None, None),
            P(("wide", "narrow"), None, None),
            P(("wide", "narrow"), None, None),
            P(("wide", "narrow"), None, None),
            P("narrow", None, None),
            P("narrow", None, None),
            P("narrow", None, None),
        ),
        out_specs=(P("wide", "narrow", None), P("wide", "narrow", None)),
        check_vma=False,
    )
```

```python
import math

import jax
import jax.numpy as jnp
from jax import lax
from jax.experimental import pallas as pl
from jax.experimental.pallas import tpu as pltpu
from jax.sharding import PartitionSpec as P

FD = 256
FHID = 512
WINDOW = 512
NS_STEPS = 5
LANES = 128
TOK = 32

coef_a = 3.4445
coef_b = -4.775
coef_c = 2.0315

XS, HALVES, YS = 4, 2, 4
PLANE = XS * YS
CUTS = (48, 80)
VMEM_LIMIT = 48 * 1024 * 1024


def dot(a, b, dims=((1,), (0,))):
    return lax.dot_general(a, b, (dims, ((), ())), preferred_element_type=jnp.float32)


def block_rows(ref, index, count):
    group = ref.shape[0]
    parts = [
        ref[:, (index + i) * TOK : (index + i + 1) * TOK, :].reshape(group * TOK, LANES)
        for i in range(count)
    ]
    return parts[0] if count == 1 else jnp.concatenate(parts, axis=1)


def gradient_kernel(first, gate, up, down, out):
    group = first.shape[0]
    span = group * TOK
    logits = first[:, 12 * TOK : 12 * TOK + 16, :].astype(jnp.float32)
    rate_blocks = []
    for source in range(group):
        turned = logits[source].T[:TOK]
        rate_blocks.append(jnp.maximum(turned, 0.0) + jnp.log1p(jnp.exp(-jnp.abs(turned))))
    rates = jnp.concatenate(rate_blocks, axis=0)
    key = block_rows(first, 4, 2)
    value = block_rows(first, 6, 2)
    gate_bf = gate[...].astype(jnp.bfloat16)
    up_bf = up[...].astype(jnp.bfloat16)
    down_bf = down[...].astype(jnp.bfloat16)
    totals = [None, None, None]
    half = span // 2
    for part in range(2):
        rows = slice(part * half, (part + 1) * half)
        key_part, value_part, rate = key[rows], value[rows], rates[rows]
        gate_pre = dot(key_part, gate_bf)
        up_pre = dot(key_part, up_bf)
        back = dot(value_part, down_bf, ((1,), (1,)))
        sigmoid_gate = 1.0 / (1.0 + jnp.exp(-gate_pre))
        activated = gate_pre * sigmoid_gate
        hidden = (activated * up_pre).astype(jnp.bfloat16)
        scaled_v = (rate[:, 1:2] * value_part.astype(jnp.float32)).astype(jnp.bfloat16)
        grad_gate = (
            rate[:, 0:1] * back * up_pre * sigmoid_gate * (1.0 + gate_pre * (1.0 - sigmoid_gate))
        ).astype(jnp.bfloat16)
        grad_up = (rate[:, 2:3] * back * activated).astype(jnp.bfloat16)
        fresh = (
            dot(key_part, grad_gate, ((0,), (0,))),
            dot(key_part, grad_up, ((0,), (0,))),
            dot(scaled_v, hidden, ((0,), (0,))),
        )
        totals = [new if old is None else old + new for old, new in zip(totals, fresh)]
    rows = FD // PLANE
    row = lax.broadcasted_iota(jnp.int32, (16, LANES), 0)
    tag = jnp.zeros((16, LANES), jnp.float32)
    for matrix, total in enumerate(totals):
        most = jnp.max(jnp.max(jnp.abs(total), axis=0, keepdims=True), axis=1, keepdims=True)
        power = jnp.floor(jnp.log(jnp.maximum(most, 1e-30)) * 1.4426950408889634)
        scaled = total * jnp.exp((13.0 - power) * 0.6931471805599453)
        tag = jnp.where(row == matrix, power, tag)
        for column in range(FHID // LANES):
            start = (matrix * (FHID // LANES) + column) * rows
            out[:, start : start + rows, :] = scaled[
                :, column * LANES : (column + 1) * LANES
            ].reshape(PLANE, rows, LANES)
    out[:, 3 * FHID // LANES * rows :, :] = jnp.broadcast_to(tag[None], (PLANE, 16, LANES))


def attention_kernel(place, first, side, edge_low, edge_mid, edge_high, out, earlier):
    span = first.shape[0] * TOK
    scale = 1.0 / math.sqrt(LANES)
    tile = 128
    reach = span + tile
    row = lax.broadcasted_iota(jnp.int32, (tile, reach), 0)
    col = lax.broadcasted_iota(jnp.int32, (tile, reach), 1)
    band = (col > row) & (col - row <= span)
    begin = jnp.where(place[0] == 0, span, 0)
    edge = lax.rem(place[0], YS) == 0
    heads = 2

    @pl.when(edge)
    def _():
        earlier[:, : CUTS[0], :] = edge_low[...]
        earlier[:, CUTS[0] : CUTS[1], :] = edge_mid[...]
        earlier[:, CUTS[1] :, :] = edge_high[...]

    @pl.when(jnp.logical_not(edge))
    def _():
        earlier[...] = side[...]

    for head in range(heads):
        query = block_rows(first, 8 + head, 1)
        key = jnp.concatenate([block_rows(earlier, head, 1), block_rows(first, head, 1)], axis=0)
        value = jnp.concatenate(
            [block_rows(earlier, heads + head, 1), block_rows(first, heads + head, 1)], axis=0
        )
        for step in range(span // tile):
            low = step * tile
            scores = dot(query[low : low + tile], key[low : low + reach], ((1,), (1,))) * scale
            keep = band & (col + low >= begin)
            scores = jnp.where(keep, scores, -1e30)
            terms = jnp.exp(scores - jnp.max(scores, axis=1, keepdims=True))
            probs = (terms * (1.0 / jnp.sum(terms, axis=1, keepdims=True))).astype(jnp.bfloat16)
            out[pl.ds(low * heads + head, tile, stride=heads), :] = dot(
                probs, value[low : low + reach]
            )


def split(a):
    high = a.astype(jnp.bfloat16)
    return high, (a - high.astype(jnp.float32)).astype(jnp.bfloat16)


def orthogonal(ortho_all):
    for _ in range(NS_STEPS):
        grams, polys, nexts = [], [], []
        halves = [split(ortho) for ortho in ortho_all]
        for high, low in halves:
            cross = dot(high, low, ((1,), (1,)))
            grams.append(dot(high, high, ((1,), (1,))) + (cross + cross.T))
        for gram in grams:
            high, low = split(gram)
            square = dot(high, high) + (dot(high, low) + dot(low, high))
            polys.append(coef_b * gram + coef_c * square)
        for ortho, poly, (high, low) in zip(ortho_all, polys, halves):
            top, rest = split(poly)
            nexts.append(coef_a * ortho + (dot(top, high) + (dot(top, low) + dot(rest, high))))
        ortho_all = nexts
    return ortho_all


def apply_kernel(powers, every, gate, up, down, first, out):
    rows = FD // PLANE
    starts = []
    for matrix in range(3):
        columns = []
        for column in range(FHID // LANES):
            start = (matrix * (FHID // LANES) + column) * rows
            columns.append(every[:, start : start + rows, :].reshape(FD, LANES))
        total = jnp.concatenate(columns, axis=1)
        squares = jnp.sum(jnp.sum(total * total, axis=0, keepdims=True), axis=1, keepdims=True)
        factor = powers[matrix : matrix + 1, 0:1]
        starts.append(total * (factor / jnp.sqrt(squares * factor * factor + 1e-6)))
    ortho = orthogonal(starts)
    new_gate = (gate[...] + ortho[0]).astype(jnp.bfloat16)
    new_up = (up[...] + ortho[1]).astype(jnp.bfloat16)
    new_down = (down[...] + ortho[2].T).astype(jnp.bfloat16)
    query = block_rows(first, 10, 2)
    gate_pre = dot(query, new_gate)
    up_pre = dot(query, new_up)
    hidden = (gate_pre * (1.0 / (1.0 + jnp.exp(-gate_pre))) * up_pre).astype(jnp.bfloat16)
    result = dot(hidden, new_down)
    span = result.shape[0]
    for column in range(FD // LANES):
        out[pl.ds(column, span, stride=FD // LANES), :] = result[
            :, column * LANES : (column + 1) * LANES
        ]


def call(kernel, shape, operands, flops, scalars=0, scratch=()):
    vmem = pl.BlockSpec(memory_space=pltpu.VMEM)
    smem = pl.BlockSpec(memory_space=pltpu.SMEM)
    return pl.pallas_call(
        kernel,
        out_shape=jax.ShapeDtypeStruct(shape, jnp.float32),
        in_specs=[smem] * scalars + [vmem] * (len(operands) - scalars),
        out_specs=vmem,
        scratch_shapes=scratch,
        compiler_params=pltpu.CompilerParams(vmem_limit_bytes=VMEM_LIMIT),
        cost_estimate=pl.CostEstimate(flops=flops, bytes_accessed=4 << 20, transcendentals=0),
    )(*operands)


def wide_index(x, half, y):
    return (x * HALVES + half) * YS + y


PLANES = [[wide_index(x, half, y) for x in range(XS) for y in range(YS)] for half in range(HALVES)]
SWAP = [
    (wide_index(x, half, y), wide_index(x, 1 - half, y))
    for x in range(XS)
    for half in range(HALVES)
    for y in range(YS)
]
AROUND = [
    (wide_index(x, half, y), wide_index(x, half, (y + 1) % YS))
    for x in range(XS)
    for half in range(HALVES)
    for y in range(YS)
]
ENDS = [(x, half, x + half, 1 - half) for x in range(XS) for half in range(HALVES)][:-1]
EDGE_LOW = [(wide_index(x, half, 0), wide_index(*after, 0)) for x, half, *after in ENDS]
EDGE_HIGH = [(wide_index(x, half, YS - 1), wide_index(*after, 0)) for x, half, *after in ENDS]
FLOPS = 1 << 20


def per_device(query_key, value_heads, fast_inputs, rate_logits, gate_fast, up_fast, down_fast):
    group = lax.axis_size("narrow")
    rows = query_key.shape[0]
    own = query_key.shape[1] // group
    span = rows * group
    pair = query_key.transpose(1, 0, 2).reshape(group, own * rows, 2 * LANES)
    value = value_heads.transpose(1, 0, 2).reshape(group, own * rows, LANES)
    fast = fast_inputs.transpose(1, 0, 2)
    fast = [fast[:, :, i * LANES : (i + 1) * LANES] for i in range(6)]
    logits = jnp.pad(rate_logits.transpose(1, 2, 0), ((0, 0), (0, 13), (0, LANES - rows)))
    first = jnp.concatenate(
        [pair[:, :, LANES:], value, *fast[2:], pair[:, :, :LANES], *fast[:2], logits], axis=1
    )
    first = lax.all_to_all(first, "narrow", 0, 0, tiled=True)
    tail = first[:, : 4 * rows]
    edge_high = lax.ppermute(first[:, CUTS[1] : 4 * rows], "wide", EDGE_HIGH)

    weights = (gate_fast[0], up_fast[0], down_fast[0])
    count = 3 * FHID // LANES * FD // PLANE
    pieces = call(gradient_kernel, (PLANE, count + 16, LANES), (first, *weights), FLOPS)
    got = lax.all_to_all(
        pieces.astype(jnp.float16), "wide", 0, 0, tiled=True, axis_index_groups=PLANES
    )
    got, tail = lax.optimization_barrier((got, tail))
    side = lax.ppermute(tail, "wide", AROUND)
    powers = got[:, count : count + 3].astype(jnp.float32)
    top = jnp.max(powers, axis=0)
    parts = got[:, :count].astype(jnp.float32).reshape(PLANE, 3, -1, LANES)
    half = jnp.sum(parts * (jnp.exp2(powers - top) * 0.0625)[:, :, None], axis=0)
    sent = jnp.concatenate(
        [half.reshape(count, LANES), top, jnp.zeros((13, LANES), jnp.float32)], axis=0
    )
    sent = sent.astype(jnp.float16)
    other = lax.ppermute(sent, "wide", SWAP)
    other, low_part, mid_part, edge_high = lax.optimization_barrier(
        (other, side[:, : CUTS[0]], tail[:, CUTS[0] : CUTS[1]], edge_high)
    )
    edge_mid = lax.ppermute(mid_part, "wide", EDGE_HIGH)
    edge_low = lax.ppermute(low_part, "wide", EDGE_LOW)
    other_top = other[count : count + 3].astype(jnp.float32)
    both = jnp.maximum(top, other_top)
    whole = half * (jnp.exp2(top - both) * 0.5)[:, None]
    whole = whole + other[:count].astype(jnp.float32).reshape(3, -1, LANES) * (
        jnp.exp2(other_top - both) * 0.5
    )[:, None]
    whole = whole.astype(jnp.float16).reshape(count, LANES)
    every = lax.all_to_all(
        jnp.broadcast_to(whole[None], (PLANE, count, LANES)),
        "wide",
        0,
        0,
        tiled=True,
        axis_index_groups=PLANES,
    )
    factors = jnp.concatenate([jnp.exp2(both - 8.0), jnp.zeros((5, LANES), jnp.float32)], axis=0)
    fast_out = call(
        apply_kernel,
        (span * FD // LANES, LANES),
        (factors, every.astype(jnp.float32), *weights, first),
        FLOPS,
    )
    place = lax.axis_index("wide").reshape(1)
    edge_low, edge_mid, fast_out = lax.optimization_barrier((edge_low, edge_mid, fast_out))
    window_out = call(
        attention_kernel,
        (span * own, LANES),
        (place, first, side, edge_low, edge_mid, edge_high),
        FLOPS,
        1,
        [pltpu.VMEM((PLANE, 4 * TOK, LANES), jnp.bfloat16)],
    )
    return (window_out.reshape(span, own, LANES), fast_out.reshape(span, 1, FD))


def solution(mesh):
    return jax.shard_map(
        per_device,
        mesh=mesh,
        in_specs=(
            P(("wide", "narrow"), None, None),
            P(("wide", "narrow"), None, None),
            P(("wide", "narrow"), None, None),
            P(("wide", "narrow"), None, None),
            P("narrow", None, None),
            P("narrow", None, None),
            P("narrow", None, None),
        ),
        out_specs=(P("wide", "narrow", None), P("wide", "narrow", None)),
        check_vma=False,
    )
```

```python
import math

import jax
import jax.numpy as jnp
from jax import lax
from jax.experimental import pallas as pl
from jax.experimental.pallas import tpu as pltpu
from jax.sharding import PartitionSpec as P

FD = 256
FHID = 512
WINDOW = 512
NS_STEPS = 5
LANES = 128
TOK = 32

coef_a = 3.4445
coef_b = -4.775
coef_c = 2.0315

XS, HALVES, YS = 4, 2, 4
PLANE = XS * YS
CUTS = (48, 96)
VMEM_LIMIT = 48 * 1024 * 1024


def dot(a, b, dims=((1,), (0,))):
    return lax.dot_general(a, b, (dims, ((), ())), preferred_element_type=jnp.float32)


def block_rows(ref, index, count):
    group = ref.shape[0]
    parts = [
        ref[:, (index + i) * TOK : (index + i + 1) * TOK, :].reshape(group * TOK, LANES)
        for i in range(count)
    ]
    return parts[0] if count == 1 else jnp.concatenate(parts, axis=1)


def gradient_kernel(first, gate, up, down, out):
    group = first.shape[0]
    span = group * TOK
    logits = first[:, 12 * TOK : 12 * TOK + 16, :].astype(jnp.float32)
    rate_blocks = []
    for source in range(group):
        turned = logits[source].T[:TOK]
        rate_blocks.append(jnp.maximum(turned, 0.0) + jnp.log1p(jnp.exp(-jnp.abs(turned))))
    rates = jnp.concatenate(rate_blocks, axis=0)
    key = block_rows(first, 4, 2)
    value = block_rows(first, 6, 2)
    gate_bf = gate[...].astype(jnp.bfloat16)
    up_bf = up[...].astype(jnp.bfloat16)
    down_bf = down[...].astype(jnp.bfloat16)
    totals = [None, None, None]
    half = span // 2
    for part in range(2):
        rows = slice(part * half, (part + 1) * half)
        key_part, value_part, rate = key[rows], value[rows], rates[rows]
        gate_pre = dot(key_part, gate_bf)
        up_pre = dot(key_part, up_bf)
        back = dot(value_part, down_bf, ((1,), (1,)))
        sigmoid_gate = 1.0 / (1.0 + jnp.exp(-gate_pre))
        activated = gate_pre * sigmoid_gate
        hidden = (activated * up_pre).astype(jnp.bfloat16)
        scaled_v = (rate[:, 1:2] * value_part.astype(jnp.float32)).astype(jnp.bfloat16)
        grad_gate = (
            rate[:, 0:1] * back * up_pre * sigmoid_gate * (1.0 + gate_pre * (1.0 - sigmoid_gate))
        ).astype(jnp.bfloat16)
        grad_up = (rate[:, 2:3] * back * activated).astype(jnp.bfloat16)
        fresh = (
            dot(key_part, grad_gate, ((0,), (0,))),
            dot(key_part, grad_up, ((0,), (0,))),
            dot(scaled_v, hidden, ((0,), (0,))),
        )
        totals = [new if old is None else old + new for old, new in zip(totals, fresh)]
    rows = FD // PLANE
    row = lax.broadcasted_iota(jnp.int32, (16, LANES), 0)
    tag = jnp.zeros((16, LANES), jnp.float32)
    for matrix, total in enumerate(totals):
        most = jnp.max(jnp.max(jnp.abs(total), axis=0, keepdims=True), axis=1, keepdims=True)
        power = jnp.floor(jnp.log(jnp.maximum(most, 1e-30)) * 1.4426950408889634)
        scaled = total * jnp.exp((13.0 - power) * 0.6931471805599453)
        tag = jnp.where(row == matrix, power, tag)
        for column in range(FHID // LANES):
            start = (matrix * (FHID // LANES) + column) * rows
            out[:, start : start + rows, :] = scaled[
                :, column * LANES : (column + 1) * LANES
            ].reshape(PLANE, rows, LANES)
    out[:, 3 * FHID // LANES * rows :, :] = jnp.broadcast_to(tag[None], (PLANE, 16, LANES))


def attention_kernel(place, first, side, edge_low, edge_mid, edge_high, out, earlier):
    span = first.shape[0] * TOK
    scale = 1.0 / math.sqrt(LANES)
    tile = 128
    reach = span + tile
    row = lax.broadcasted_iota(jnp.int32, (tile, reach), 0)
    col = lax.broadcasted_iota(jnp.int32, (tile, reach), 1)
    band = (col > row) & (col - row <= span)
    begin = jnp.where(place[0] == 0, span, 0)
    edge = lax.rem(place[0], YS) == 0
    heads = 2

    @pl.when(edge)
    def _():
        earlier[:, : CUTS[0], :] = edge_low[...]
        earlier[:, CUTS[0] : CUTS[1], :] = edge_mid[...]
        earlier[:, CUTS[1] :, :] = edge_high[...]

    @pl.when(jnp.logical_not(edge))
    def _():
        earlier[...] = side[...]

    for head in range(heads):
        query = block_rows(first, 8 + head, 1)
        key = jnp.concatenate([block_rows(earlier, head, 1), block_rows(first, head, 1)], axis=0)
        value = jnp.concatenate(
            [block_rows(earlier, heads + head, 1), block_rows(first, heads + head, 1)], axis=0
        )
        for step in range(span // tile):
            low = step * tile
            scores = dot(query[low : low + tile], key[low : low + reach], ((1,), (1,))) * scale
            keep = band & (col + low >= begin)
            scores = jnp.where(keep, scores, -1e30)
            terms = jnp.exp(scores - jnp.max(scores, axis=1, keepdims=True))
            probs = (terms * (1.0 / jnp.sum(terms, axis=1, keepdims=True))).astype(jnp.bfloat16)
            out[pl.ds(low * heads + head, tile, stride=heads), :] = dot(
                probs, value[low : low + reach]
            )


def split(a):
    high = a.astype(jnp.bfloat16)
    return high, (a - high.astype(jnp.float32)).astype(jnp.bfloat16)


def orthogonal(ortho_all):
    for _ in range(NS_STEPS):
        grams, polys, nexts = [], [], []
        halves = [split(ortho) for ortho in ortho_all]
        for high, low in halves:
            cross = dot(high, low, ((1,), (1,)))
            grams.append(dot(high, high, ((1,), (1,))) + (cross + cross.T))
        for gram in grams:
            high, low = split(gram)
            square = dot(high, high) + (dot(high, low) + dot(low, high))
            polys.append(coef_b * gram + coef_c * square)
        for ortho, poly, (high, low) in zip(ortho_all, polys, halves):
            top, rest = split(poly)
            nexts.append(coef_a * ortho + (dot(top, high) + (dot(top, low) + dot(rest, high))))
        ortho_all = nexts
    return ortho_all


def apply_kernel(powers, every, gate, up, down, first, out):
    rows = FD // PLANE
    starts = []
    for matrix in range(3):
        columns = []
        for column in range(FHID // LANES):
            start = (matrix * (FHID // LANES) + column) * rows
            columns.append(every[:, start : start + rows, :].reshape(FD, LANES))
        total = jnp.concatenate(columns, axis=1)
        squares = jnp.sum(jnp.sum(total * total, axis=0, keepdims=True), axis=1, keepdims=True)
        factor = powers[matrix : matrix + 1, 0:1]
        starts.append(total * (factor / jnp.sqrt(squares * factor * factor + 1e-6)))
    ortho = orthogonal(starts)
    new_gate = (gate[...] + ortho[0]).astype(jnp.bfloat16)
    new_up = (up[...] + ortho[1]).astype(jnp.bfloat16)
    new_down = (down[...] + ortho[2].T).astype(jnp.bfloat16)
    query = block_rows(first, 10, 2)
    gate_pre = dot(query, new_gate)
    up_pre = dot(query, new_up)
    hidden = (gate_pre * (1.0 / (1.0 + jnp.exp(-gate_pre))) * up_pre).astype(jnp.bfloat16)
    result = dot(hidden, new_down)
    span = result.shape[0]
    for column in range(FD // LANES):
        out[pl.ds(column, span, stride=FD // LANES), :] = result[
            :, column * LANES : (column + 1) * LANES
        ]


def call(kernel, shape, operands, flops, scalars=0, scratch=()):
    vmem = pl.BlockSpec(memory_space=pltpu.VMEM)
    smem = pl.BlockSpec(memory_space=pltpu.SMEM)
    return pl.pallas_call(
        kernel,
        out_shape=jax.ShapeDtypeStruct(shape, jnp.float32),
        in_specs=[smem] * scalars + [vmem] * (len(operands) - scalars),
        out_specs=vmem,
        scratch_shapes=scratch,
        compiler_params=pltpu.CompilerParams(vmem_limit_bytes=VMEM_LIMIT),
        cost_estimate=pl.CostEstimate(flops=flops, bytes_accessed=4 << 20, transcendentals=0),
    )(*operands)


def wide_index(x, half, y):
    return (x * HALVES + half) * YS + y


PLANES = [[wide_index(x, half, y) for x in range(XS) for y in range(YS)] for half in range(HALVES)]
SWAP = [
    (wide_index(x, half, y), wide_index(x, 1 - half, y))
    for x in range(XS)
    for half in range(HALVES)
    for y in range(YS)
]
AROUND = [
    (wide_index(x, half, y), wide_index(x, half, (y + 1) % YS))
    for x in range(XS)
    for half in range(HALVES)
    for y in range(YS)
]
ENDS = [(x, half, x + half, 1 - half) for x in range(XS) for half in range(HALVES)][:-1]
EDGE_LOW = [(wide_index(x, half, 0), wide_index(*after, 0)) for x, half, *after in ENDS]
EDGE_HIGH = [(wide_index(x, half, YS - 1), wide_index(*after, 0)) for x, half, *after in ENDS]
FLOPS = 1 << 20


def per_device(query_key, value_heads, fast_inputs, rate_logits, gate_fast, up_fast, down_fast):
    group = lax.axis_size("narrow")
    rows = query_key.shape[0]
    own = query_key.shape[1] // group
    span = rows * group
    pair = query_key.transpose(1, 0, 2).reshape(group, own * rows, 2 * LANES)
    value = value_heads.transpose(1, 0, 2).reshape(group, own * rows, LANES)
    fast = fast_inputs.transpose(1, 0, 2)
    fast = [fast[:, :, i * LANES : (i + 1) * LANES] for i in range(6)]
    logits = jnp.pad(rate_logits.transpose(1, 2, 0), ((0, 0), (0, 13), (0, LANES - rows)))
    first = jnp.concatenate(
        [pair[:, :, LANES:], value, *fast[2:], pair[:, :, :LANES], *fast[:2], logits], axis=1
    )
    first = lax.all_to_all(first, "narrow", 0, 0, tiled=True)
    tail = first[:, : 4 * rows]
    edge_high = lax.ppermute(first[:, CUTS[1] : 4 * rows], "wide", EDGE_HIGH)

    weights = (gate_fast[0], up_fast[0], down_fast[0])
    count = 3 * FHID // LANES * FD // PLANE
    pieces = call(gradient_kernel, (PLANE, count + 16, LANES), (first, *weights), FLOPS)
    got = lax.all_to_all(
        pieces.astype(jnp.float16), "wide", 0, 0, tiled=True, axis_index_groups=PLANES
    )
    got, tail = lax.optimization_barrier((got, tail))
    side = lax.ppermute(tail, "wide", AROUND)
    powers = got[:, count : count + 3].astype(jnp.float32)
    top = jnp.max(powers, axis=0)
    parts = got[:, :count].astype(jnp.float32).reshape(PLANE, 3, -1, LANES)
    half = jnp.sum(parts * (jnp.exp2(powers - top) * 0.0625)[:, :, None], axis=0)
    sent = jnp.concatenate(
        [half.reshape(count, LANES), top, jnp.zeros((13, LANES), jnp.float32)], axis=0
    )
    sent = sent.astype(jnp.float16)
    other = lax.ppermute(sent, "wide", SWAP)
    other, low_part, mid_part, edge_high = lax.optimization_barrier(
        (other, side[:, : CUTS[0]], tail[:, CUTS[0] : CUTS[1]], edge_high)
    )
    edge_mid = lax.ppermute(mid_part, "wide", EDGE_HIGH)
    edge_low = lax.ppermute(low_part, "wide", EDGE_LOW)
    other_top = other[count : count + 3].astype(jnp.float32)
    both = jnp.maximum(top, other_top)
    whole = half * (jnp.exp2(top - both) * 0.5)[:, None]
    whole = whole + other[:count].astype(jnp.float32).reshape(3, -1, LANES) * (
        jnp.exp2(other_top - both) * 0.5
    )[:, None]
    whole = whole.astype(jnp.float16).reshape(count, LANES)
    every = lax.all_to_all(
        jnp.broadcast_to(whole[None], (PLANE, count, LANES)),
        "wide",
        0,
        0,
        tiled=True,
        axis_index_groups=PLANES,
    )
    factors = jnp.concatenate([jnp.exp2(both - 8.0), jnp.zeros((5, LANES), jnp.float32)], axis=0)
    fast_out = call(
        apply_kernel,
        (span * FD // LANES, LANES),
        (factors, every.astype(jnp.float32), *weights, first),
        FLOPS,
    )
    place = lax.axis_index("wide").reshape(1)
    edge_low, edge_mid, fast_out = lax.optimization_barrier((edge_low, edge_mid, fast_out))
    window_out = call(
        attention_kernel,
        (span * own, LANES),
        (place, first, side, edge_low, edge_mid, edge_high),
        FLOPS,
        1,
        [pltpu.VMEM((PLANE, 4 * TOK, LANES), jnp.bfloat16)],
    )
    return (window_out.reshape(span, own, LANES), fast_out.reshape(span, 1, FD))


def solution(mesh):
    return jax.shard_map(
        per_device,
        mesh=mesh,
        in_specs=(
            P(("wide", "narrow"), None, None),
            P(("wide", "narrow"), None, None),
            P(("wide", "narrow"), None, None),
            P(("wide", "narrow"), None, None),
            P("narrow", None, None),
            P("narrow", None, None),
            P("narrow", None, None),
        ),
        out_specs=(P("wide", "narrow", None), P("wide", "narrow", None)),
        check_vma=False,
    )
```

```python
import math

import jax
import jax.numpy as jnp
from jax import lax
from jax.experimental import pallas as pl
from jax.experimental.pallas import tpu as pltpu
from jax.sharding import PartitionSpec as P

FD = 256
FHID = 512
WINDOW = 512
NS_STEPS = 5
LANES = 128
TOK = 32

coef_a = 3.4445
coef_b = -4.775
coef_c = 2.0315

XS, HALVES, YS = 4, 2, 4
PLANE = XS * YS
CUTS = (64, 80)
VMEM_LIMIT = 48 * 1024 * 1024


def dot(a, b, dims=((1,), (0,))):
    return lax.dot_general(a, b, (dims, ((), ())), preferred_element_type=jnp.float32)


def block_rows(ref, index, count):
    group = ref.shape[0]
    parts = [
        ref[:, (index + i) * TOK : (index + i + 1) * TOK, :].reshape(group * TOK, LANES)
        for i in range(count)
    ]
    return parts[0] if count == 1 else jnp.concatenate(parts, axis=1)


def gradient_kernel(first, gate, up, down, out):
    group = first.shape[0]
    span = group * TOK
    logits = first[:, 12 * TOK : 12 * TOK + 16, :].astype(jnp.float32)
    rate_blocks = []
    for source in range(group):
        turned = logits[source].T[:TOK]
        rate_blocks.append(jnp.maximum(turned, 0.0) + jnp.log1p(jnp.exp(-jnp.abs(turned))))
    rates = jnp.concatenate(rate_blocks, axis=0)
    key = block_rows(first, 4, 2)
    value = block_rows(first, 6, 2)
    gate_bf = gate[...].astype(jnp.bfloat16)
    up_bf = up[...].astype(jnp.bfloat16)
    down_bf = down[...].astype(jnp.bfloat16)
    totals = [None, None, None]
    half = span // 2
    for part in range(2):
        rows = slice(part * half, (part + 1) * half)
        key_part, value_part, rate = key[rows], value[rows], rates[rows]
        gate_pre = dot(key_part, gate_bf)
        up_pre = dot(key_part, up_bf)
        back = dot(value_part, down_bf, ((1,), (1,)))
        sigmoid_gate = 1.0 / (1.0 + jnp.exp(-gate_pre))
        activated = gate_pre * sigmoid_gate
        hidden = (activated * up_pre).astype(jnp.bfloat16)
        scaled_v = (rate[:, 1:2] * value_part.astype(jnp.float32)).astype(jnp.bfloat16)
        grad_gate = (
            rate[:, 0:1] * back * up_pre * sigmoid_gate * (1.0 + gate_pre * (1.0 - sigmoid_gate))
        ).astype(jnp.bfloat16)
        grad_up = (rate[:, 2:3] * back * activated).astype(jnp.bfloat16)
        fresh = (
            dot(key_part, grad_gate, ((0,), (0,))),
            dot(key_part, grad_up, ((0,), (0,))),
            dot(scaled_v, hidden, ((0,), (0,))),
        )
        totals = [new if old is None else old + new for old, new in zip(totals, fresh)]
    rows = FD // PLANE
    row = lax.broadcasted_iota(jnp.int32, (16, LANES), 0)
    tag = jnp.zeros((16, LANES), jnp.float32)
    for matrix, total in enumerate(totals):
        most = jnp.max(jnp.max(jnp.abs(total), axis=0, keepdims=True), axis=1, keepdims=True)
        power = jnp.floor(jnp.log(jnp.maximum(most, 1e-30)) * 1.4426950408889634)
        scaled = total * jnp.exp((13.0 - power) * 0.6931471805599453)
        tag = jnp.where(row == matrix, power, tag)
        for column in range(FHID // LANES):
            start = (matrix * (FHID // LANES) + column) * rows
            out[:, start : start + rows, :] = scaled[
                :, column * LANES : (column + 1) * LANES
            ].reshape(PLANE, rows, LANES)
    out[:, 3 * FHID // LANES * rows :, :] = jnp.broadcast_to(tag[None], (PLANE, 16, LANES))


def attention_kernel(place, first, side, edge_low, edge_mid, edge_high, out, earlier):
    span = first.shape[0] * TOK
    scale = 1.0 / math.sqrt(LANES)
    tile = 128
    reach = span + tile
    row = lax.broadcasted_iota(jnp.int32, (tile, reach), 0)
    col = lax.broadcasted_iota(jnp.int32, (tile, reach), 1)
    band = (col > row) & (col - row <= span)
    begin = jnp.where(place[0] == 0, span, 0)
    edge = lax.rem(place[0], YS) == 0
    heads = 2

    @pl.when(edge)
    def _():
        earlier[:, : CUTS[0], :] = edge_low[...]
        earlier[:, CUTS[0] : CUTS[1], :] = edge_mid[...]
        earlier[:, CUTS[1] :, :] = edge_high[...]

    @pl.when(jnp.logical_not(edge))
    def _():
        earlier[...] = side[...]

    for head in range(heads):
        query = block_rows(first, 8 + head, 1)
        key = jnp.concatenate([block_rows(earlier, head, 1), block_rows(first, head, 1)], axis=0)
        value = jnp.concatenate(
            [block_rows(earlier, heads + head, 1), block_rows(first, heads + head, 1)], axis=0
        )
        for step in range(span // tile):
            low = step * tile
            scores = dot(query[low : low + tile], key[low : low + reach], ((1,), (1,))) * scale
            keep = band & (col + low >= begin)
            scores = jnp.where(keep, scores, -1e30)
            terms = jnp.exp(scores - jnp.max(scores, axis=1, keepdims=True))
            probs = (terms * (1.0 / jnp.sum(terms, axis=1, keepdims=True))).astype(jnp.bfloat16)
            out[pl.ds(low * heads + head, tile, stride=heads), :] = dot(
                probs, value[low : low + reach]
            )


def split(a):
    high = a.astype(jnp.bfloat16)
    return high, (a - high.astype(jnp.float32)).astype(jnp.bfloat16)


def orthogonal(ortho_all):
    for _ in range(NS_STEPS):
        grams, polys, nexts = [], [], []
        halves = [split(ortho) for ortho in ortho_all]
        for high, low in halves:
            cross = dot(high, low, ((1,), (1,)))
            grams.append(dot(high, high, ((1,), (1,))) + (cross + cross.T))
        for gram in grams:
            high, low = split(gram)
            square = dot(high, high) + (dot(high, low) + dot(low, high))
            polys.append(coef_b * gram + coef_c * square)
        for ortho, poly, (high, low) in zip(ortho_all, polys, halves):
            top, rest = split(poly)
            nexts.append(coef_a * ortho + (dot(top, high) + (dot(top, low) + dot(rest, high))))
        ortho_all = nexts
    return ortho_all


def apply_kernel(powers, every, gate, up, down, first, out):
    rows = FD // PLANE
    starts = []
    for matrix in range(3):
        columns = []
        for column in range(FHID // LANES):
            start = (matrix * (FHID // LANES) + column) * rows
            columns.append(every[:, start : start + rows, :].reshape(FD, LANES))
        total = jnp.concatenate(columns, axis=1)
        squares = jnp.sum(jnp.sum(total * total, axis=0, keepdims=True), axis=1, keepdims=True)
        factor = powers[matrix : matrix + 1, 0:1]
        starts.append(total * (factor / jnp.sqrt(squares * factor * factor + 1e-6)))
    ortho = orthogonal(starts)
    new_gate = (gate[...] + ortho[0]).astype(jnp.bfloat16)
    new_up = (up[...] + ortho[1]).astype(jnp.bfloat16)
    new_down = (down[...] + ortho[2].T).astype(jnp.bfloat16)
    query = block_rows(first, 10, 2)
    gate_pre = dot(query, new_gate)
    up_pre = dot(query, new_up)
    hidden = (gate_pre * (1.0 / (1.0 + jnp.exp(-gate_pre))) * up_pre).astype(jnp.bfloat16)
    result = dot(hidden, new_down)
    span = result.shape[0]
    for column in range(FD // LANES):
        out[pl.ds(column, span, stride=FD // LANES), :] = result[
            :, column * LANES : (column + 1) * LANES
        ]


def call(kernel, shape, operands, flops, scalars=0, scratch=()):
    vmem = pl.BlockSpec(memory_space=pltpu.VMEM)
    smem = pl.BlockSpec(memory_space=pltpu.SMEM)
    return pl.pallas_call(
        kernel,
        out_shape=jax.ShapeDtypeStruct(shape, jnp.float32),
        in_specs=[smem] * scalars + [vmem] * (len(operands) - scalars),
        out_specs=vmem,
        scratch_shapes=scratch,
        compiler_params=pltpu.CompilerParams(vmem_limit_bytes=VMEM_LIMIT),
        cost_estimate=pl.CostEstimate(flops=flops, bytes_accessed=4 << 20, transcendentals=0),
    )(*operands)


def wide_index(x, half, y):
    return (x * HALVES + half) * YS + y


PLANES = [[wide_index(x, half, y) for x in range(XS) for y in range(YS)] for half in range(HALVES)]
SWAP = [
    (wide_index(x, half, y), wide_index(x, 1 - half, y))
    for x in range(XS)
    for half in range(HALVES)
    for y in range(YS)
]
AROUND = [
    (wide_index(x, half, y), wide_index(x, half, (y + 1) % YS))
    for x in range(XS)
    for half in range(HALVES)
    for y in range(YS)
]
ENDS = [(x, half, x + half, 1 - half) for x in range(XS) for half in range(HALVES)][:-1]
EDGE_LOW = [(wide_index(x, half, 0), wide_index(*after, 0)) for x, half, *after in ENDS]
EDGE_HIGH = [(wide_index(x, half, YS - 1), wide_index(*after, 0)) for x, half, *after in ENDS]
FLOPS = 1 << 20


def per_device(query_key, value_heads, fast_inputs, rate_logits, gate_fast, up_fast, down_fast):
    group = lax.axis_size("narrow")
    rows = query_key.shape[0]
    own = query_key.shape[1] // group
    span = rows * group
    pair = query_key.transpose(1, 0, 2).reshape(group, own * rows, 2 * LANES)
    value = value_heads.transpose(1, 0, 2).reshape(group, own * rows, LANES)
    fast = fast_inputs.transpose(1, 0, 2)
    fast = [fast[:, :, i * LANES : (i + 1) * LANES] for i in range(6)]
    logits = jnp.pad(rate_logits.transpose(1, 2, 0), ((0, 0), (0, 13), (0, LANES - rows)))
    first = jnp.concatenate(
        [pair[:, :, LANES:], value, *fast[2:], pair[:, :, :LANES], *fast[:2], logits], axis=1
    )
    first = lax.all_to_all(first, "narrow", 0, 0, tiled=True)
    tail = first[:, : 4 * rows]
    edge_high = lax.ppermute(first[:, CUTS[1] : 4 * rows], "wide", EDGE_HIGH)

    weights = (gate_fast[0], up_fast[0], down_fast[0])
    count = 3 * FHID // LANES * FD // PLANE
    pieces = call(gradient_kernel, (PLANE, count + 16, LANES), (first, *weights), FLOPS)
    got = lax.all_to_all(
        pieces.astype(jnp.float16), "wide", 0, 0, tiled=True, axis_index_groups=PLANES
    )
    got, tail = lax.optimization_barrier((got, tail))
    side = lax.ppermute(tail, "wide", AROUND)
    powers = got[:, count : count + 3].astype(jnp.float32)
    top = jnp.max(powers, axis=0)
    parts = got[:, :count].astype(jnp.float32).reshape(PLANE, 3, -1, LANES)
    half = jnp.sum(parts * (jnp.exp2(powers - top) * 0.0625)[:, :, None], axis=0)
    sent = jnp.concatenate(
        [half.reshape(count, LANES), top, jnp.zeros((13, LANES), jnp.float32)], axis=0
    )
    sent = sent.astype(jnp.float16)
    other = lax.ppermute(sent, "wide", SWAP)
    other, low_part, mid_part, edge_high = lax.optimization_barrier(
        (other, side[:, : CUTS[0]], tail[:, CUTS[0] : CUTS[1]], edge_high)
    )
    edge_mid = lax.ppermute(mid_part, "wide", EDGE_HIGH)
    edge_low = lax.ppermute(low_part, "wide", EDGE_LOW)
    other_top = other[count : count + 3].astype(jnp.float32)
    both = jnp.maximum(top, other_top)
    whole = half * (jnp.exp2(top - both) * 0.5)[:, None]
    whole = whole + other[:count].astype(jnp.float32).reshape(3, -1, LANES) * (
        jnp.exp2(other_top - both) * 0.5
    )[:, None]
    whole = whole.astype(jnp.float16).reshape(count, LANES)
    every = lax.all_to_all(
        jnp.broadcast_to(whole[None], (PLANE, count, LANES)),
        "wide",
        0,
        0,
        tiled=True,
        axis_index_groups=PLANES,
    )
    factors = jnp.concatenate([jnp.exp2(both - 8.0), jnp.zeros((5, LANES), jnp.float32)], axis=0)
    fast_out = call(
        apply_kernel,
        (span * FD // LANES, LANES),
        (factors, every.astype(jnp.float32), *weights, first),
        FLOPS,
    )
    place = lax.axis_index("wide").reshape(1)
    edge_low, edge_mid, fast_out = lax.optimization_barrier((edge_low, edge_mid, fast_out))
    window_out = call(
        attention_kernel,
        (span * own, LANES),
        (place, first, side, edge_low, edge_mid, edge_high),
        FLOPS,
        1,
        [pltpu.VMEM((PLANE, 4 * TOK, LANES), jnp.bfloat16)],
    )
    return (window_out.reshape(span, own, LANES), fast_out.reshape(span, 1, FD))


def solution(mesh):
    return jax.shard_map(
        per_device,
        mesh=mesh,
        in_specs=(
            P(("wide", "narrow"), None, None),
            P(("wide", "narrow"), None, None),
            P(("wide", "narrow"), None, None),
            P(("wide", "narrow"), None, None),
            P("narrow", None, None),
            P("narrow", None, None),
            P("narrow", None, None),
        ),
        out_specs=(P("wide", "narrow", None), P("wide", "narrow", None)),
        check_vma=False,
    )
```
